256 devices in a mesh: ctx: 8 (over x, core), grp: 32 (over y, z).
Axes of the slice: x: 4, y: 4, z: 8, core: 2. Of those that a mesh axis runs over, the one named last changes fastest.
Arguments:
- queries: bfloat16 [32, 1024, 8192], P('grp', 'ctx'), may hold values from -32 to 32
- keys: bfloat16 [32, 1024, 1024], P('grp', 'ctx'), may hold values from -32 to 32
- values: bfloat16 [32, 1024, 1024], P('grp', 'ctx'), may hold values from -6 to 6
- placement: int32 [32, 16], P('grp', 'ctx'), may hold values from 0 to 15, each once within a row
- lengths: int32 [32], replicated, may hold values from 1 to 32, 512 in all
Outputs:
- attended: bfloat16 [32, 1024, 8192], P('grp', 'ctx')
The draws below stay inside these ranges and needn't reach their ends.
Inputs may be any that keep to these rules, and one draw needn't show every extreme that they name: `placement`: every row is a permutation of the stretches of its column. `lengths`: the entries sum to 512; some request takes exactly 32 stretches.
All inputs are finite; a program needn't handle non-finite values.
Results may differ from the reference program's by a relative error of at most 0.005.
Values may be sent and summed in bfloat16 or wider, within the bound.
A program may use at most 256 MiB of HBM per device.

```python
import math
import jax
import jax.numpy as jnp
import numpy as np
from jax import lax

QH = 64
KVH = 8
HD = 128
STRETCH = 64
CPD = 2
SPAN = 3
COL = 1024
REQS = 32
N_CTX = 8
N_GRP = 32


def draw_keys(key, part):
    key = jax.random.fold_in(key, 7)
    column_rows = N_CTX * CPD * STRETCH
    base_keys = jax.random.normal(key, (N_GRP, column_rows, KVH, HD), jnp.float32)
    return jnp.clip(base_keys, -32.0, 32.0).reshape(N_GRP, column_rows, KVH * HD).astype(jnp.bfloat16)


def draw_queries(key, part):
    key = jax.random.fold_in(key, 9)
    column_rows = N_CTX * CPD * STRETCH
    base_query = jax.random.normal(key, (N_GRP, column_rows, KVH, QH // KVH, HD), jnp.float32)
    return jnp.clip(base_query, -32.0, 32.0).reshape(N_GRP, column_rows, QH * HD).astype(jnp.bfloat16)


def block_levels(key, extent, pieces, low, largest):
    def one(dim, blocks):
        heights = jax.random.uniform(jax.random.fold_in(jax.random.fold_in(key, 6), dim), (blocks,), jnp.float32, low / len(pieces), largest / len(pieces))
        return jnp.repeat(jnp.exp(heights), extent[dim] // blocks).reshape((-1,) + (1,) * (len(extent) - dim - 1))

    gain = one(*pieces[0])
    for cut in pieces[1:]:
        gain = gain * one(*cut)
    return gain


def profile(count, total, limit, skew):
    loads = [(1 << 20) // math.isqrt(rank ** skew) + 1 for rank in range(2, count + 1)]
    rest, given = total - limit - (count - 1), [1] * (count - 1)
    while rest > 0:
        free = [i for i in range(count - 1) if given[i] < limit]
        pool, left = sum([loads[i] for i in free]), rest
        for i in free:
            extra = min(limit - given[i], max(1, left * loads[i] // pool), rest)
            given[i] = given[i] + extra
            rest = rest - extra
    return np.array([limit] + given)


def ragged_sizes(own_key, count, total, limit, slope):
    if count == 2:
        one = jax.random.randint(own_key, (), max(1, total - limit), min(limit, total - 1) + 1)
        return jnp.stack([one, total - one])
    tallies = jnp.asarray(profile(count, total, limit, slope), jnp.int32)
    twos = (count - 1) // 2
    giver, receiver = tallies[1:1 + 2 * twos:2], tallies[2:2 + 2 * twos:2]
    margin = jnp.minimum(giver - 1, limit - receiver)
    shifted = jax.random.randint(jax.random.fold_in(own_key, 1), (twos,), 0, 1 << 20) % (margin + 1)
    tallies = tallies.at[1:1 + 2 * twos:2].set(giver - shifted).at[2:2 + 2 * twos:2].set(receiver + shifted)
    return tallies[jax.random.permutation(jax.random.fold_in(own_key, 2), count)]


def bell_draw(key, shape, deviation, reach, cuts=(), kind=jnp.bfloat16):
    level = block_levels(key, shape, cuts, -0.22, 0.18) if cuts else 1.0
    values = jax.random.normal(key, shape, jnp.float32) * deviation * level
    return jnp.minimum(jnp.maximum(values, -reach), reach).astype(kind)


def setup_inputs(seed: int = 0) -> dict:
    splits = jax.random.split(jax.random.key(seed), 6)
    return {
        "queries": draw_queries(jax.random.fold_in(splits[5], 71), 0),
        "keys": draw_keys(jax.random.fold_in(splits[5], 71), 0),
        "values": bell_draw(splits[2], (N_GRP, COL, KVH * HD), 1.0, 6.0, ((0, 32), (1, 8))),
        "placement": jax.vmap(lambda own: jax.random.permutation(own, N_CTX * CPD))(jax.random.split(splits[3], N_GRP)).reshape((N_GRP, N_CTX * CPD)).astype(jnp.int32),
        "lengths": ragged_sizes(splits[4], REQS, N_GRP * N_CTX * CPD, (SPAN - 1) * N_CTX * CPD, 0).astype(jnp.int32),
    }


NEG = -1e+30

def reference(queries, keys, values, placement, lengths):
    column_rows = N_CTX * CPD * STRETCH
    tok_rows = CPD * STRETCH
    groups = QH // KVH
    req_ends = jnp.cumsum(lengths).astype(jnp.int32)
    columns = jnp.arange(N_GRP, dtype=jnp.int32)
    within = jnp.arange(column_rows, dtype=jnp.int32)
    tok_pos = (columns[:, None] * column_rows + jnp.repeat(placement, STRETCH, axis=1) * STRETCH + within[None, :] % STRETCH).astype(jnp.int32)
    tok_stretch = tok_pos // STRETCH
    tok_req = lax.optimization_barrier(jnp.sum((req_ends[None, None, :] <= tok_stretch[:, :, None]).astype(jnp.int32), axis=2)).astype(jnp.int32)
    front = SPAN - 1
    pad_keys = jnp.concatenate([jnp.zeros((front, column_rows, KVH * HD), keys.dtype), keys], 0)
    pad_values = jnp.concatenate([jnp.zeros((front, column_rows, KVH * HD), values.dtype), values], 0)
    pad_pos = jnp.concatenate([jnp.zeros((front, column_rows), jnp.int32), tok_pos], 0)
    pad_req = jnp.concatenate([jnp.full((front, column_rows), -1, jnp.int32), tok_req], 0)
    zero_idx = jnp.zeros((), jnp.int32)

    def one_block(index):
        column = (index // N_CTX).astype(jnp.int32)
        shard = (index % N_CTX).astype(jnp.int32)
        first = (shard * tok_rows).astype(jnp.int32)
        q_rows = lax.dynamic_slice(queries, (column, first, zero_idx), (1, tok_rows, QH * HD))[0]
        q_pos = lax.dynamic_slice(tok_pos, (column, first), (1, tok_rows))[0]
        q_req = lax.dynamic_slice(tok_req, (column, first), (1, tok_rows))[0]
        k_rows = lax.dynamic_slice(pad_keys, (column, zero_idx, zero_idx), (SPAN, column_rows, KVH * HD))
        v_rows = lax.dynamic_slice(pad_values, (column, zero_idx, zero_idx), (SPAN, column_rows, KVH * HD))
        k_rows = k_rows.reshape(SPAN * column_rows, KVH, HD).astype(jnp.float32)
        v_rows = v_rows.reshape(SPAN * column_rows, KVH, HD).astype(jnp.float32)
        k_pos = lax.dynamic_slice(pad_pos, (column, zero_idx), (SPAN, column_rows)).reshape(SPAN * column_rows)
        k_req = lax.dynamic_slice(pad_req, (column, zero_idx), (SPAN, column_rows)).reshape(SPAN * column_rows)
        visible = (k_req[None, :] == q_req[:, None]) & (k_pos[None, :] <= q_pos[:, None])
        q_four = q_rows.reshape(tok_rows, KVH, groups, HD).astype(jnp.float32)
        scores = jnp.einsum('qhgd,khd->hgqk', q_four, k_rows) / math.sqrt(HD)
        masked = visible[None, None]
        row_max = lax.optimization_barrier(jnp.max(jnp.where(masked, scores, NEG), axis=-1, keepdims=True))
        weights = jnp.where(masked, jnp.exp(scores - row_max), 0.0)
        row_sum = lax.optimization_barrier(jnp.sum(weights, axis=-1))
        rounded = lax.optimization_barrier(weights.astype(jnp.bfloat16)).astype(jnp.float32)
        mixed = jnp.einsum('hgqk,khd->qhgd', rounded, v_rows)
        result = mixed / jnp.transpose(row_sum, (2, 0, 1))[..., None]
        return result.reshape(tok_rows, QH * HD).astype(jnp.bfloat16)
    blocks = lax.map(one_block, jnp.arange(N_GRP * N_CTX, dtype=jnp.int32))
    return blocks.reshape(N_GRP, column_rows, QH * HD)
```

```python
import functools
import math

import jax
import jax.numpy as jnp
from jax import lax
from jax.experimental import pallas as pl
from jax.experimental.pallas import tpu as pltpu
from jax.sharding import PartitionSpec as P

HD = 128
KVH = 8
GROUPS = 8
STRETCH = 64
TOK = 128
COL_STRETCHES = 16
REQS = 32
NUM_X = 4
NUM_GRP = 32
ROWS = GROUPS * TOK
TILE = 512
MAX_KEYS = 768

NEG = -1e30
HIDDEN = -2e30
MESH = pl.DeviceIdType.MESH
K, V, POS = 0, 1, 2


def kernel(q_hbm, k_hbm, v_hbm, place_ref, len_ref, out_ref,
           kbuf, vbuf, pbuf, q_vm, qs, acc, run_max, bias,
           local_sem, recv_ici, recv_sib, send_z, send_x, send_fwd, send_sib):
    ctx = lax.axis_index("ctx")
    grp = lax.axis_index("grp")
    x = ctx // 2
    core = ctx % 2
    right = (((x + 1) % NUM_X) * 2 + core, grp)
    left = (((x + NUM_X - 1) % NUM_X) * 2 + core, grp)
    sibling = (x * 2 + 1 - core, grp)
    after = (ctx, (grp + 1) % NUM_GRP)
    before = (ctx, (grp + NUM_GRP - 1) % NUM_GRP)
    bufs = (kbuf, vbuf, pbuf)

    local = [
        pltpu.make_async_copy(k_hbm.at[0], kbuf.at[0, 0, 0], local_sem.at[0]),
        pltpu.make_async_copy(v_hbm.at[0], vbuf.at[0, 0, 0], local_sem.at[1]),
        pltpu.make_async_copy(q_hbm.at[0], q_vm, local_sem.at[2]),
    ]
    for copy in local:
        copy.start()

    first = grp * COL_STRETCHES + place_ref[0, 0]
    second = grp * COL_STRETCHES + place_ref[0, 1]
    end = jnp.int32(0)
    start_first = jnp.int32(0)
    start_second = jnp.int32(0)
    for r in range(REQS):
        end = end + len_ref[r]
        start_first = jnp.where(end <= first, end, start_first)
        start_second = jnp.where(end <= second, end, start_second)

    def by_token(shape, dim, of_first, of_second, step):
        token = lax.broadcasted_iota(jnp.int32, shape, dim)
        within = token % STRETCH
        return jnp.where(token < STRETCH, of_first, of_second) * STRETCH + within * step

    pbuf[0, 0, 0] = by_token((8, TOK), 1, first, second, 1)

    barrier = pltpu.get_barrier_semaphore()
    for device in (right, left, sibling, after, before):
        pl.semaphore_signal(barrier, inc=1, device_id=device, device_id_type=MESH)
    pl.semaphore_wait(barrier, 5)

    started = []

    def send(kind, src, d, rx, side, sem, device):
        recv = (recv_sib if side else recv_ici).at[d, rx, kind]
        copy = pltpu.make_async_remote_copy(
            src_ref=src, dst_ref=bufs[kind].at[d, rx, side],
            send_sem=sem, recv_sem=recv, device_id=device, device_id_type=MESH)
        copy.start()
        started.append(copy)

    def held(kind, d, rx):
        if d == 0 and rx == 0 and kind != POS:
            return (k_hbm, v_hbm)[kind].at[0]
        return bufs[kind].at[d, rx, 0]

    def to_sibling(d, rx, kinds=(POS, K, V)):
        for kind in kinds:
            send(kind, held(kind, d, rx), d, rx, 1, send_sib.at[d, rx, kind], sibling)

    def to_after(d):
        for kind in (POS, K, V):
            send(kind, held(kind, d, 0), d + 1, 0, 0, send_z.at[d, kind], after)

    def along_x(d):
        send(POS, held(POS, d, 0), d, 1, 0, send_x.at[d, 0, POS], right)
        send(POS, held(POS, d, 0), d, 2, 0, send_x.at[d, 1, POS], left)
        send(K, held(K, d, 0), d, 1, 0, send_x.at[d, 0, K], right)
        send(V, held(V, d, 0), d, 2, 0, send_x.at[d, 1, V], left)
        send(V, held(V, d, 0), d, 1, 0, send_x.at[d, 0, V], right)
        send(K, held(K, d, 0), d, 2, 0, send_x.at[d, 1, K], left)

    def forward_x(d):
        send(POS, held(POS, d, 1), d, 3, 0, send_fwd.at[d, POS], right)
        send(K, held(K, d, 1), d, 3, 0, send_fwd.at[d, K], right)
        send(V, held(V, d, 2), d, 3, 0, send_fwd.at[d, V], left)

    def arrived(d, rx, kinds=(POS, K, V), side=0):
        for kind in kinds:
            ref = bufs[kind].at[d, rx, side]
            recv = (recv_sib if side else recv_ici).at[d, rx, kind]
            pltpu.make_async_remote_copy(
                src_ref=ref, dst_ref=ref, send_sem=local_sem.at[3], recv_sem=recv,
                device_id=sibling, device_id_type=MESH).wait_recv()

    def events_first_hop(d):
        arrived(d, 1, (POS, K))
        arrived(d, 2, (POS, V))
        forward_x(d)
        to_sibling(d, 1, (POS, K))
        to_sibling(d, 2, (POS, V))

    def events_rest(d):
        arrived(d, 1, (V,))
        arrived(d, 2, (K,))
        to_sibling(d, 1, (V,))
        to_sibling(d, 2, (K,))

    def events_opposite(d):
        arrived(d, 3)
        to_sibling(d, 3)

    def events_column(d):
        arrived(d, 0)
        if d < 2:
            to_after(d)
        along_x(d)
        to_sibling(d, 0)

    def attend(chunks, is_first=False, is_last=False):
        pieces = [(d, rx, side) for d, rx in chunks for side in range(2)]
        num_keys = TOK * len(pieces)
        key_pos = jnp.concatenate([pbuf[d, rx, side, 0:1, :] for d, rx, side in pieces], axis=1)
        query_pos = by_token((TOK, 1), 0, first, second, 1)
        query_start = by_token((TOK, 1), 0, start_first, start_second, 0)
        visible = (key_pos >= query_start) & (key_pos <= query_pos)
        bias[:, :num_keys] = jnp.where(visible, 0.0, HIDDEN)

        def one_head(head, carry):
            lanes = pl.ds(pl.multiple_of(head * HD, HD), HD)
            keys = jnp.concatenate([kbuf[d, rx, side, :, lanes] for d, rx, side in pieces], axis=0)
            vals = jnp.concatenate([vbuf[d, rx, side, :, lanes] for d, rx, side in pieces], axis=0)
            keys = jnp.concatenate([keys, keys], axis=1)
            vals = jnp.concatenate([vals, jnp.ones_like(vals)], axis=1)
            hidden = bias[:, :num_keys]
            scores = []
            for t in range(ROWS // TILE):
                rows = slice(t * TILE, (t + 1) * TILE)
                scores.append(lax.dot_general(
                    qs[head, rows], keys, (((1,), (1,)), ((), ())),
                    preferred_element_type=jnp.float32))
            for t in range(ROWS // TILE):
                rows = slice(t * TILE, (t + 1) * TILE)
                masked = scores[t].reshape(TILE // TOK, TOK, num_keys) + hidden[None]
                masked = masked.reshape(TILE, num_keys)
                top = jnp.max(masked, axis=1, keepdims=True)
                if not is_first:
                    old = run_max[head, rows]
                    top = jnp.maximum(old[:, 0:1], top)
                weights = jnp.exp2(masked - top).astype(jnp.bfloat16)
                part = lax.dot_general(
                    weights, vals, (((1,), (0,)), ((), ())),
                    preferred_element_type=jnp.float32)
                if not is_first:
                    factor = jnp.exp2(old - top)
                    part = part + acc[head, rows] * jnp.concatenate([factor, factor], axis=1)
                if is_last:
                    result = (part[:, :HD] / part[:, HD:]).astype(jnp.bfloat16)
                    for j in range(TILE // TOK):
                        group = t * (TILE // TOK) + j
                        place = pl.ds(pl.multiple_of((head * GROUPS + group) * HD, HD), HD)
                        out_ref[0, :, place] = result[j * TOK:(j + 1) * TOK]
                else:
                    acc[head, rows] = part
                    run_max[head, rows] = jnp.broadcast_to(top, (TILE, HD))
            return carry

        lax.fori_loop(0, KVH, one_head, 0)

    to_sibling(0, 0)
    to_after(0)
    along_x(0)

    local[2].wait()

    def prepare(head, carry):
        for group in range(GROUPS):
            lanes = pl.ds(pl.multiple_of((head * GROUPS + group) * HD, HD), HD)
            scaled = q_vm[:, lanes].astype(jnp.float32) * (math.log2(math.e) / math.sqrt(HD))
            high = scaled.astype(jnp.bfloat16)
            low = (scaled - high.astype(jnp.float32)).astype(jnp.bfloat16)
            qs[head, group * TOK:(group + 1) * TOK, :HD] = high
            qs[head, group * TOK:(group + 1) * TOK, HD:] = low
        return carry

    lax.fori_loop(0, KVH, prepare, 0)
    local[0].wait()
    local[1].wait()
    arrived(0, 0, side=1)
    attend([(0, 0)], is_first=True)

    events_first_hop(0)
    events_column(1)
    events_rest(0)
    for rx in (1, 2):
        arrived(0, rx, side=1)
    arrived(1, 0, side=1)
    attend([(0, 1), (0, 2), (1, 0)])

    events_opposite(0)
    events_column(2)
    events_first_hop(1)
    arrived(0, 3, side=1)
    arrived(2, 0, side=1)
    attend([(0, 3), (2, 0)])

    events_rest(1)
    for rx in (1, 2):
        arrived(1, rx, side=1)
    attend([(1, 1), (1, 2)])

    events_opposite(1)
    events_first_hop(2)
    arrived(1, 3, side=1)
    attend([(1, 3)])

    events_rest(2)
    for rx in (1, 2):
        arrived(2, rx, side=1)
    attend([(2, 1), (2, 2)])

    events_opposite(2)
    arrived(2, 3, side=1)
    attend([(2, 3)], is_last=True)

    for copy in started:
        copy.wait_send()


def body(queries, keys, values, placement, lengths):
    any_spec = pl.BlockSpec(memory_space=pl.ANY)
    smem = pl.BlockSpec(memory_space=pltpu.SMEM)
    dma = pltpu.SemaphoreType.DMA
    return pl.pallas_call(
        kernel,
        out_shape=jax.ShapeDtypeStruct((1, TOK, KVH * GROUPS * HD), jnp.bfloat16),
        in_specs=[any_spec, any_spec, any_spec, smem, smem],
        out_specs=pl.BlockSpec(memory_space=pltpu.VMEM),
        scratch_shapes=[
            pltpu.VMEM((3, NUM_X, 2, TOK, KVH * HD), jnp.bfloat16),
            pltpu.VMEM((3, NUM_X, 2, TOK, KVH * HD), jnp.bfloat16),
            pltpu.VMEM((3, NUM_X, 2, 8, TOK), jnp.int32),
            pltpu.VMEM((TOK, KVH * GROUPS * HD), jnp.bfloat16),
            pltpu.VMEM((KVH, ROWS, 2 * HD), jnp.bfloat16),
            pltpu.VMEM((KVH, ROWS, 2 * HD), jnp.float32),
            pltpu.VMEM((KVH, ROWS, HD), jnp.float32),
            pltpu.VMEM((TOK, MAX_KEYS), jnp.float32),
            dma((4,)),
            dma((3, NUM_X, 3)),
            dma((3, NUM_X, 3)),
            dma((2, 3)),
            dma((3, 2, 3)),
            dma((3, 3)),
            dma((3, NUM_X, 3)),
        ],
        compiler_params=pltpu.CompilerParams(
            collective_id=0, has_side_effects=True, vmem_limit_bytes=56 * 1024 * 1024),
        cost_estimate=pl.CostEstimate(
            flops=4 * TOK * 64 * 3072 * HD, bytes_accessed=5 * 1024 * 1024,
            transcendentals=TOK * 64 * 3072),
    )(queries, keys, values, placement, lengths)


def solution(mesh):
    in_specs = (
        P("grp", "ctx", None),
        P("grp", "ctx", None),
        P("grp", "ctx", None),
        P("grp", "ctx"),
        P(),
    )
    out_specs = P("grp", "ctx", None)
    return jax.shard_map(body, mesh=mesh, in_specs=in_specs, out_specs=out_specs, check_vma=False)
```

```python
import functools
import math

import jax
import jax.numpy as jnp
from jax import lax
from jax.experimental import pallas as pl
from jax.experimental.pallas import tpu as pltpu
from jax.sharding import PartitionSpec as P

HD = 128
KVH = 8
GROUPS = 8
STRETCH = 64
TOK = 128
COL_STRETCHES = 16
REQS = 32
NUM_X = 4
NUM_GRP = 32
ROWS = GROUPS * TOK
TILE = 512
MAX_KEYS = 768

HIDDEN = -2e30
SCALE = math.log2(math.e) / math.sqrt(HD)
MESH = pl.DeviceIdType.MESH
K, V, POS = 0, 1, 2


def kernel(q_hbm, k_hbm, v_hbm, place_ref, len_ref, out_ref,
           kbuf, vbuf, pbuf, q_vm, qs, acc, run_max, extra,
           local_sem, recv_ici, recv_sib, send_z, send_x, send_fwd, send_sib):
    ctx = lax.axis_index("ctx")
    grp = lax.axis_index("grp")
    x = ctx // 2
    core = ctx % 2
    right = (((x + 1) % NUM_X) * 2 + core, grp)
    left = (((x + NUM_X - 1) % NUM_X) * 2 + core, grp)
    sibling = (x * 2 + 1 - core, grp)
    after = (ctx, (grp + 1) % NUM_GRP)
    before = (ctx, (grp + NUM_GRP - 1) % NUM_GRP)
    bufs = (kbuf, vbuf, pbuf)

    local = [
        pltpu.make_async_copy(k_hbm.at[0], kbuf.at[0, 0, 0], local_sem.at[0]),
        pltpu.make_async_copy(v_hbm.at[0], vbuf.at[0, 0, 0], local_sem.at[1]),
        pltpu.make_async_copy(q_hbm.at[0], q_vm, local_sem.at[2]),
    ]
    for copy in local:
        copy.start()

    first = grp * COL_STRETCHES + place_ref[0, 0]
    second = grp * COL_STRETCHES + place_ref[0, 1]
    end = jnp.int32(0)
    start_first = jnp.int32(0)
    start_second = jnp.int32(0)
    for r in range(REQS):
        end = end + len_ref[r]
        start_first = jnp.where(end <= first, end, start_first)
        start_second = jnp.where(end <= second, end, start_second)

    pbuf[0, 0, 0, 0:8] = jnp.full((8, TOK), first, jnp.int32)
    pbuf[0, 0, 0, 8:16] = jnp.full((8, TOK), second, jnp.int32)

    barrier = pltpu.get_barrier_semaphore()
    for device in (right, left, sibling, after, before):
        pl.semaphore_signal(barrier, inc=1, device_id=device, device_id_type=MESH)
    pl.semaphore_wait(barrier, 5)

    started = []

    def send(kind, src, d, rx, side, sem, device):
        recv = (recv_sib if side else recv_ici).at[d, rx, kind]
        copy = pltpu.make_async_remote_copy(
            src_ref=src, dst_ref=bufs[kind].at[d, rx, side],
            send_sem=sem, recv_sem=recv, device_id=device, device_id_type=MESH)
        copy.start()
        started.append(copy)

    def held(kind, d, rx):
        if d == 0 and rx == 0 and kind != POS:
            return (k_hbm, v_hbm)[kind].at[0]
        return bufs[kind].at[d, rx, 0]

    def to_sibling(d, rx, kinds=(POS, K, V)):
        for kind in kinds:
            send(kind, held(kind, d, rx), d, rx, 1, send_sib.at[d, rx, kind], sibling)

    def to_after(d):
        for kind in (POS, K, V):
            send(kind, held(kind, d, 0), d + 1, 0, 0, send_z.at[d, kind], after)

    def along_x(d):
        send(POS, held(POS, d, 0), d, 1, 0, send_x.at[d, 0, POS], right)
        send(POS, held(POS, d, 0), d, 2, 0, send_x.at[d, 1, POS], left)
        send(K, held(K, d, 0), d, 1, 0, send_x.at[d, 0, K], right)
        send(V, held(V, d, 0), d, 2, 0, send_x.at[d, 1, V], left)
        send(V, held(V, d, 0), d, 1, 0, send_x.at[d, 0, V], right)
        send(K, held(K, d, 0), d, 2, 0, send_x.at[d, 1, K], left)

    def forward_x(d):
        send(POS, held(POS, d, 1), d, 3, 0, send_fwd.at[d, POS], right)
        send(K, held(K, d, 1), d, 3, 0, send_fwd.at[d, K], right)
        send(V, held(V, d, 2), d, 3, 0, send_fwd.at[d, V], left)

    def arrived(d, rx, kinds=(POS, K, V), side=0):
        for kind in kinds:
            ref = bufs[kind].at[d, rx, side]
            recv = (recv_sib if side else recv_ici).at[d, rx, kind]
            pltpu.make_async_remote_copy(
                src_ref=ref, dst_ref=ref, send_sem=local_sem.at[3], recv_sem=recv,
                device_id=sibling, device_id_type=MESH).wait_recv()

    def events_first_hop(d):
        arrived(d, 1, (POS, K))
        arrived(d, 2, (POS, V))
        forward_x(d)
        to_sibling(d, 1, (POS, K))
        to_sibling(d, 2, (POS, V))

    def events_rest(d):
        arrived(d, 1, (V,))
        arrived(d, 2, (K,))
        to_sibling(d, 1, (V,))
        to_sibling(d, 2, (K,))

    def events_opposite(d):
        arrived(d, 3)
        to_sibling(d, 3)

    def events_column(d):
        arrived(d, 0)
        if d < 2:
            to_after(d)
        along_x(d)
        to_sibling(d, 0)

    def causal():
        row = lax.broadcasted_iota(jnp.int32, (TOK, TOK), 0)
        col = lax.broadcasted_iota(jnp.int32, (TOK, TOK), 1)
        later = (row // STRETCH == col // STRETCH) & (col > row)
        return jnp.where(later, HIDDEN, 0.0)

    def attend(chunks, is_first=False, is_last=False):
        pieces = [(d, rx, side) for d, rx in chunks for side in range(2)]
        num_keys = TOK * len(pieces)
        lane = lax.broadcasted_iota(jnp.int32, (8, HD), 1)
        for i, (d, rx, side) in enumerate(pieces):
            for half in range(2):
                stretch = pbuf[d, rx, side, 8 * half:8 * half + 8, :]
                seen_first = (stretch >= start_first) & (stretch <= first)
                seen_second = (stretch >= start_second) & (stretch <= second)
                seen = jnp.where(lane == 0, seen_first.astype(jnp.int32), seen_second.astype(jnp.int32))
                hide = jnp.where(seen == 1, 0.0, HIDDEN)
                row = i * TOK + half * STRETCH
                extra[row:row + STRETCH, :] = jnp.concatenate([hide] * 8, axis=0).astype(jnp.bfloat16)

        def one_head(head, carry):
            lanes = pl.ds(pl.multiple_of(head * HD, HD), HD)
            keys = jnp.concatenate([kbuf[d, rx, side, :, lanes] for d, rx, side in pieces], axis=0)
            vals = jnp.concatenate([vbuf[d, rx, side, :, lanes] for d, rx, side in pieces], axis=0)
            keys = jnp.concatenate([keys, extra[:num_keys, :]], axis=1)
            vals = jnp.concatenate([vals, jnp.ones_like(vals)], axis=1)
            scores = []
            for t in range(ROWS // TILE):
                rows = slice(t * TILE, (t + 1) * TILE)
                scores.append(lax.dot_general(
                    qs[head, rows], keys, (((1,), (1,)), ((), ())),
                    preferred_element_type=jnp.float32))
            for t in range(ROWS // TILE):
                rows = slice(t * TILE, (t + 1) * TILE)
                masked = scores[t]
                if is_first:
                    own = masked[:, :TOK].reshape(TILE // TOK, TOK, TOK) + causal()[None]
                    masked = jnp.concatenate([own.reshape(TILE, TOK), masked[:, TOK:]], axis=1)
                top = jnp.max(masked, axis=1, keepdims=True)
                if not is_first:
                    old = run_max[head, rows]
                    top = jnp.maximum(old[:, 0:1], top)
                weights = jnp.exp2((masked - top) * SCALE).astype(jnp.bfloat16)
                part = lax.dot_general(
                    weights, vals, (((1,), (0,)), ((), ())),
                    preferred_element_type=jnp.float32)
                if not is_first:
                    factor = jnp.exp2((old - top) * SCALE)
                    part = part + acc[head, rows] * jnp.concatenate([factor, factor], axis=1)
                if is_last:
                    result = (part[:, :HD] / part[:, HD:]).astype(jnp.bfloat16)
                    for j in range(TILE // TOK):
                        group = t * (TILE // TOK) + j
                        place = pl.ds(pl.multiple_of((head * GROUPS + group) * HD, HD), HD)
                        out_ref[0, :, place] = result[j * TOK:(j + 1) * TOK]
                else:
                    acc[head, rows] = part
                    run_max[head, rows] = jnp.broadcast_to(top, (TILE, HD))
            return carry

        lax.fori_loop(0, KVH, one_head, 0)

    to_sibling(0, 0)
    to_after(0)
    along_x(0)

    local[2].wait()

    row = lax.broadcasted_iota(jnp.int32, (TOK, HD), 0)
    col = lax.broadcasted_iota(jnp.int32, (TOK, HD), 1)
    which = jnp.where(row // STRETCH == col, 1.0, 0.0).astype(jnp.bfloat16)

    def prepare(head, carry):
        for group in range(GROUPS):
            lanes = pl.ds(pl.multiple_of((head * GROUPS + group) * HD, HD), HD)
            qs[head, group * TOK:(group + 1) * TOK, :HD] = q_vm[:, lanes]
            qs[head, group * TOK:(group + 1) * TOK, HD:] = which
        return carry

    lax.fori_loop(0, KVH, prepare, 0)
    local[0].wait()
    local[1].wait()
    arrived(0, 0, side=1)
    attend([(0, 0)], is_first=True)

    events_first_hop(0)
    events_column(1)
    events_rest(0)
    for rx in (1, 2):
        arrived(0, rx, side=1)
    arrived(1, 0, side=1)
    attend([(0, 1), (0, 2), (1, 0)])

    events_opposite(0)
    events_column(2)
    events_first_hop(1)
    arrived(0, 3, side=1)
    arrived(2, 0, side=1)
    attend([(0, 3), (2, 0)])

    events_rest(1)
    for rx in (1, 2):
        arrived(1, rx, side=1)
    attend([(1, 1), (1, 2)])

    events_opposite(1)
    events_first_hop(2)
    arrived(1, 3, side=1)
    attend([(1, 3)])

    events_rest(2)
    for rx in (1, 2):
        arrived(2, rx, side=1)
    attend([(2, 1), (2, 2)])

    events_opposite(2)
    arrived(2, 3, side=1)
    attend([(2, 3)], is_last=True)

    for copy in started:
        copy.wait_send()


def body(queries, keys, values, placement, lengths):
    any_spec = pl.BlockSpec(memory_space=pl.ANY)
    smem = pl.BlockSpec(memory_space=pltpu.SMEM)
    dma = pltpu.SemaphoreType.DMA
    return pl.pallas_call(
        kernel,
        out_shape=jax.ShapeDtypeStruct((1, TOK, KVH * GROUPS * HD), jnp.bfloat16),
        in_specs=[any_spec, any_spec, any_spec, smem, smem],
        out_specs=pl.BlockSpec(memory_space=pltpu.VMEM),
        scratch_shapes=[
            pltpu.VMEM((3, NUM_X, 2, TOK, KVH * HD), jnp.bfloat16),
            pltpu.VMEM((3, NUM_X, 2, TOK, KVH * HD), jnp.bfloat16),
            pltpu.VMEM((3, NUM_X, 2, 16, TOK), jnp.int32),
            pltpu.VMEM((TOK, KVH * GROUPS * HD), jnp.bfloat16),
            pltpu.VMEM((KVH, ROWS, 2 * HD), jnp.bfloat16),
            pltpu.VMEM((KVH, ROWS, 2 * HD), jnp.float32),
            pltpu.VMEM((KVH, ROWS, HD), jnp.float32),
            pltpu.VMEM((MAX_KEYS, HD), jnp.bfloat16),
            dma((4,)),
            dma((3, NUM_X, 3)),
            dma((3, NUM_X, 3)),
            dma((2, 3)),
            dma((3, 2, 3)),
            dma((3, 3)),
            dma((3, NUM_X, 3)),
        ],
        compiler_params=pltpu.CompilerParams(
            collective_id=0, has_side_effects=True, vmem_limit_bytes=56 * 1024 * 1024),
        cost_estimate=pl.CostEstimate(
            flops=4 * TOK * 64 * 3072 * HD, bytes_accessed=5 * 1024 * 1024,
            transcendentals=TOK * 64 * 3072),
    )(queries, keys, values, placement, lengths)


def solution(mesh):
    in_specs = (
        P("grp", "ctx", None),
        P("grp", "ctx", None),
        P("grp", "ctx", None),
        P("grp", "ctx"),
        P(),
    )
    out_specs = P("grp", "ctx", None)
    return jax.shard_map(body, mesh=mesh, in_specs=in_specs, out_specs=out_specs, check_vma=False)
```

```python
import functools
import math

import jax
import jax.numpy as jnp
from jax import lax
from jax.experimental import pallas as pl
from jax.experimental.pallas import tpu as pltpu
from jax.sharding import PartitionSpec as P

HD = 128
KVH = 8
GROUPS = 8
STRETCH = 64
TOK = 128
COL_STRETCHES = 16
REQS = 32
NUM_X = 4
NUM_GRP = 32
ROWS = GROUPS * TOK
TILE = 512
MAX_KEYS = 768
HEADS_AT_ONCE = 2

HIDDEN = -2e30
SCALE = math.log2(math.e) / math.sqrt(HD)
MESH = pl.DeviceIdType.MESH
K, V, POS = 0, 1, 2


def kernel(q_hbm, k_hbm, v_hbm, place_ref, len_ref, out_ref,
           kbuf, vbuf, pbuf, q_vm, qs, acc, run_max, extra,
           local_sem, recv_ici, recv_sib, send_z, send_x, send_fwd, send_sib):
    ctx = lax.axis_index("ctx")
    grp = lax.axis_index("grp")
    x = ctx // 2
    core = ctx % 2
    right = (((x + 1) % NUM_X) * 2 + core, grp)
    left = (((x + NUM_X - 1) % NUM_X) * 2 + core, grp)
    sibling = (x * 2 + 1 - core, grp)
    after = (ctx, (grp + 1) % NUM_GRP)
    before = (ctx, (grp + NUM_GRP - 1) % NUM_GRP)
    bufs = (kbuf, vbuf, pbuf)

    local = [
        pltpu.make_async_copy(k_hbm.at[0], kbuf.at[0, 0, 0], local_sem.at[0]),
        pltpu.make_async_copy(v_hbm.at[0], vbuf.at[0, 0, 0], local_sem.at[1]),
        pltpu.make_async_copy(q_hbm.at[0], q_vm, local_sem.at[2]),
    ]
    for copy in local:
        copy.start()

    first = grp * COL_STRETCHES + place_ref[0, 0]
    second = grp * COL_STRETCHES + place_ref[0, 1]
    end = jnp.int32(0)
    start_first = jnp.int32(0)
    start_second = jnp.int32(0)
    for r in range(REQS):
        end = end + len_ref[r]
        start_first = jnp.where(end <= first, end, start_first)
        start_second = jnp.where(end <= second, end, start_second)

    pbuf[0, 0, 0, 0:8] = jnp.full((8, TOK), first, jnp.int32)
    pbuf[0, 0, 0, 8:16] = jnp.full((8, TOK), second, jnp.int32)

    barrier = pltpu.get_barrier_semaphore()
    for device in (right, left, sibling, after, before):
        pl.semaphore_signal(barrier, inc=1, device_id=device, device_id_type=MESH)
    pl.semaphore_wait(barrier, 5)

    started = []

    def send(kind, src, d, rx, side, sem, device):
        recv = (recv_sib if side else recv_ici).at[d, rx, kind]
        copy = pltpu.make_async_remote_copy(
            src_ref=src, dst_ref=bufs[kind].at[d, rx, side],
            send_sem=sem, recv_sem=recv, device_id=device, device_id_type=MESH)
        copy.start()
        started.append(copy)

    def held(kind, d, rx):
        if d == 0 and rx == 0 and kind != POS:
            return (k_hbm, v_hbm)[kind].at[0]
        return bufs[kind].at[d, rx, 0]

    def to_sibling(d, rx, kinds=(POS, K, V)):
        for kind in kinds:
            send(kind, held(kind, d, rx), d, rx, 1, send_sib.at[d, rx, kind], sibling)

    def to_after(d):
        for kind in (POS, K, V):
            send(kind, held(kind, d, 0), d + 1, 0, 0, send_z.at[d, kind], after)

    def along_x(d):
        send(POS, held(POS, d, 0), d, 1, 0, send_x.at[d, 0, POS], right)
        send(POS, held(POS, d, 0), d, 2, 0, send_x.at[d, 1, POS], left)
        send(K, held(K, d, 0), d, 1, 0, send_x.at[d, 0, K], right)
        send(V, held(V, d, 0), d, 2, 0, send_x.at[d, 1, V], left)
        send(V, held(V, d, 0), d, 1, 0, send_x.at[d, 0, V], right)
        send(K, held(K, d, 0), d, 2, 0, send_x.at[d, 1, K], left)

    def forward_x(d):
        send(POS, held(POS, d, 1), d, 3, 0, send_fwd.at[d, POS], right)
        send(K, held(K, d, 1), d, 3, 0, send_fwd.at[d, K], right)
        send(V, held(V, d, 2), d, 3, 0, send_fwd.at[d, V], left)

    def arrived(d, rx, kinds=(POS, K, V), side=0):
        for kind in kinds:
            ref = bufs[kind].at[d, rx, side]
            recv = (recv_sib if side else recv_ici).at[d, rx, kind]
            pltpu.make_async_remote_copy(
                src_ref=ref, dst_ref=ref, send_sem=local_sem.at[3], recv_sem=recv,
                device_id=sibling, device_id_type=MESH).wait_recv()

    def events_first_hop(d):
        arrived(d, 1, (POS, K))
        arrived(d, 2, (POS, V))
        forward_x(d)
        to_sibling(d, 1, (POS, K))
        to_sibling(d, 2, (POS, V))

    def events_rest(d):
        arrived(d, 1, (V,))
        arrived(d, 2, (K,))
        to_sibling(d, 1, (V,))
        to_sibling(d, 2, (K,))

    def events_opposite(d):
        arrived(d, 3)
        to_sibling(d, 3)

    def events_column(d):
        arrived(d, 0)
        if d < 2:
            to_after(d)
        along_x(d)
        to_sibling(d, 0)

    def causal():
        row = lax.broadcasted_iota(jnp.int32, (TOK, TOK), 0)
        col = lax.broadcasted_iota(jnp.int32, (TOK, TOK), 1)
        later = (row // STRETCH == col // STRETCH) & (col > row)
        return jnp.where(later, HIDDEN, 0.0)

    def attend(chunks, is_first=False, is_last=False):
        pieces = [(d, rx, side) for d, rx in chunks for side in range(2)]
        num_keys = TOK * len(pieces)
        lane = lax.broadcasted_iota(jnp.int32, (8, HD), 1)
        for i, (d, rx, side) in enumerate(pieces):
            for half in range(2):
                stretch = pbuf[d, rx, side, 8 * half:8 * half + 8, :]
                seen_first = (stretch >= start_first) & (stretch <= first)
                seen_second = (stretch >= start_second) & (stretch <= second)
                seen = jnp.where(lane == 0, seen_first.astype(jnp.int32), seen_second.astype(jnp.int32))
                hide = jnp.where(seen == 1, 0.0, HIDDEN)
                row = i * TOK + half * STRETCH
                extra[row:row + STRETCH, :] = jnp.concatenate([hide] * 8, axis=0).astype(jnp.bfloat16)

        def load(head):
            lanes = pl.ds(pl.multiple_of(head * HD, HD), HD)
            keys = jnp.concatenate([kbuf[d, rx, side, :, lanes] for d, rx, side in pieces], axis=0)
            vals = jnp.concatenate([vbuf[d, rx, side, :, lanes] for d, rx, side in pieces], axis=0)
            keys = jnp.concatenate([keys, extra[:num_keys, :]], axis=1)
            vals = jnp.concatenate([vals, jnp.ones_like(vals)], axis=1)
            return head, keys, vals

        def score(loaded, rows):
            head, keys, _ = loaded
            return lax.dot_general(
                qs[head, rows], keys, (((1,), (1,)), ((), ())),
                preferred_element_type=jnp.float32)

        def absorb(loaded, rows, scores):
            head, _, vals = loaded
            if is_first:
                own = scores[:, :TOK].reshape(TILE // TOK, TOK, TOK) + causal()[None]
                scores = jnp.concatenate([own.reshape(TILE, TOK), scores[:, TOK:]], axis=1)
            top = jnp.broadcast_to(jnp.max(scores, axis=1, keepdims=True), (TILE, HD)) * SCALE
            if not is_first:
                old = run_max[head, rows]
                top = jnp.maximum(old, top)
            tops = jnp.concatenate([top] * (num_keys // HD), axis=1)
            weights = jnp.exp2(scores * SCALE - tops).astype(jnp.bfloat16)
            part = lax.dot_general(
                weights, vals, (((1,), (0,)), ((), ())),
                preferred_element_type=jnp.float32)
            if not is_first:
                factor = jnp.exp2(old - top)
                part = part + acc[head, rows] * jnp.concatenate([factor, factor], axis=1)
            if is_last:
                result = (part[:, :HD] / part[:, HD:]).astype(jnp.bfloat16)
                for j in range(TILE // TOK):
                    group = rows.start // TOK + j
                    place = pl.ds(pl.multiple_of((head * GROUPS + group) * HD, HD), HD)
                    out_ref[0, :, place] = result[j * TOK:(j + 1) * TOK]
            else:
                acc[head, rows] = part
                run_max[head, rows] = top

        def some_heads(step, carry):
            work = []
            for i in range(HEADS_AT_ONCE):
                loaded = load(step * HEADS_AT_ONCE + i)
                work += [(loaded, slice(t, t + TILE)) for t in range(0, ROWS, TILE)]
            scores = score(*work[0])
            for i, (loaded, rows) in enumerate(work):
                following = score(*work[i + 1]) if i + 1 < len(work) else None
                absorb(loaded, rows, scores)
                scores = following
            return carry

        lax.fori_loop(0, KVH // HEADS_AT_ONCE, some_heads, 0)

    to_sibling(0, 0)
    to_after(0)
    along_x(0)

    local[2].wait()

    row = lax.broadcasted_iota(jnp.int32, (TOK, HD), 0)
    col = lax.broadcasted_iota(jnp.int32, (TOK, HD), 1)
    which = jnp.where(row // STRETCH == col, 1.0, 0.0).astype(jnp.bfloat16)

    def prepare(head, carry):
        for group in range(GROUPS):
            lanes = pl.ds(pl.multiple_of((head * GROUPS + group) * HD, HD), HD)
            qs[head, group * TOK:(group + 1) * TOK, :HD] = q_vm[:, lanes]
            qs[head, group * TOK:(group + 1) * TOK, HD:] = which
        return carry

    lax.fori_loop(0, KVH, prepare, 0)
    local[0].wait()
    local[1].wait()
    arrived(0, 0, side=1)
    attend([(0, 0)], is_first=True)

    events_first_hop(0)
    events_column(1)
    events_rest(0)
    for rx in (1, 2):
        arrived(0, rx, side=1)
    arrived(1, 0, side=1)
    attend([(0, 1), (0, 2), (1, 0)])

    events_opposite(0)
    events_column(2)
    events_first_hop(1)
    arrived(0, 3, side=1)
    arrived(2, 0, side=1)
    attend([(0, 3), (2, 0)])

    events_rest(1)
    for rx in (1, 2):
        arrived(1, rx, side=1)
    attend([(1, 1), (1, 2)])

    events_opposite(1)
    events_first_hop(2)
    arrived(1, 3, side=1)
    attend([(1, 3)])

    events_rest(2)
    for rx in (1, 2):
        arrived(2, rx, side=1)
    attend([(2, 1), (2, 2)])

    events_opposite(2)
    arrived(2, 3, side=1)
    attend([(2, 3)], is_last=True)

    for copy in started:
        copy.wait_send()


def body(queries, keys, values, placement, lengths):
    any_spec = pl.BlockSpec(memory_space=pl.ANY)
    smem = pl.BlockSpec(memory_space=pltpu.SMEM)
    dma = pltpu.SemaphoreType.DMA
    return pl.pallas_call(
        kernel,
        out_shape=jax.ShapeDtypeStruct((1, TOK, KVH * GROUPS * HD), jnp.bfloat16),
        in_specs=[any_spec, any_spec, any_spec, smem, smem],
        out_specs=pl.BlockSpec(memory_space=pltpu.VMEM),
        scratch_shapes=[
            pltpu.VMEM((3, NUM_X, 2, TOK, KVH * HD), jnp.bfloat16),
            pltpu.VMEM((3, NUM_X, 2, TOK, KVH * HD), jnp.bfloat16),
            pltpu.VMEM((3, NUM_X, 2, 16, TOK), jnp.int32),
            pltpu.VMEM((TOK, KVH * GROUPS * HD), jnp.bfloat16),
            pltpu.VMEM((KVH, ROWS, 2 * HD), jnp.bfloat16),
            pltpu.VMEM((KVH, ROWS, 2 * HD), jnp.float32),
            pltpu.VMEM((KVH, ROWS, HD), jnp.float32),
            pltpu.VMEM((MAX_KEYS, HD), jnp.bfloat16),
            dma((4,)),
            dma((3, NUM_X, 3)),
            dma((3, NUM_X, 3)),
            dma((2, 3)),
            dma((3, 2, 3)),
            dma((3, 3)),
            dma((3, NUM_X, 3)),
        ],
        compiler_params=pltpu.CompilerParams(
            collective_id=0, has_side_effects=True, vmem_limit_bytes=56 * 1024 * 1024),
        cost_estimate=pl.CostEstimate(
            flops=4 * TOK * 64 * 3072 * HD, bytes_accessed=5 * 1024 * 1024,
            transcendentals=TOK * 64 * 3072),
    )(queries, keys, values, placement, lengths)


def solution(mesh):
    in_specs = (
        P("grp", "ctx", None),
        P("grp", "ctx", None),
        P("grp", "ctx", None),
        P("grp", "ctx"),
        P(),
    )
    out_specs = P("grp", "ctx", None)
    return jax.shard_map(body, mesh=mesh, in_specs=in_specs, out_specs=out_specs, check_vma=False)
```

```python
import math

import jax
import jax.numpy as jnp
from jax import lax
from jax.experimental import pallas as pl
from jax.experimental.pallas import tpu as pltpu
from jax.sharding import PartitionSpec as P

HD = 128
KVH = 8
GROUPS = 8
STRETCH = 64
TOK = 128
COL_STRETCHES = 16
REQS = 32
NUM_X = 4
NUM_GRP = 32
ROWS = GROUPS * TOK
TILE = 512
HALF_HEADS = 4
HALF_LANES = HALF_HEADS * HD
HEADS_AT_ONCE = 2
MAX_KEYS = 512
COPY_PARTS = TOK // 16
SUM_ROWS = 16
ACC_ROWS = HD + SUM_ROWS
OUT_LANES = HEADS_AT_ONCE * GROUPS * HD
NUM_OUT = KVH // HEADS_AT_ONCE

HIDDEN = -2e30
SCALE = math.log2(math.e) / math.sqrt(HD)
MESH = pl.DeviceIdType.MESH
H0, H1, POS = 0, 1, 2


def kernel(q_hbm, k_hbm, v_hbm, place_ref, len_ref, out_hbm,
           kvbuf, pbuf, q_vm, out_vm, acc, run_max, extra,
           local_sem, out_sem, recv_ici, recv_sib, send_z, send_x, send_sib):
    ctx = lax.axis_index("ctx")
    grp = lax.axis_index("grp")
    x = ctx // 2
    core = ctx % 2
    right = (((x + 1) % NUM_X) * 2 + core, grp)
    left = (((x + NUM_X - 1) % NUM_X) * 2 + core, grp)
    sibling = (x * 2 + 1 - core, grp)
    after = (ctx, (grp + 1) % NUM_GRP)
    before = (ctx, (grp + NUM_GRP - 1) % NUM_GRP)

    local = []
    for half in range(2):
        lanes = slice(half * HALF_LANES, (half + 1) * HALF_LANES)
        for part, source in enumerate((k_hbm, v_hbm)):
            local.append(pltpu.make_async_copy(
                source.at[0, :, lanes], kvbuf.at[0, 0, 0, half, part], local_sem.at[half, part]))
    queries_in = pltpu.make_async_copy(q_hbm.at[0], q_vm, local_sem.at[2, 0])
    for copy in local + [queries_in]:
        copy.start()

    first = grp * COL_STRETCHES + place_ref[0, 0]
    second = grp * COL_STRETCHES + place_ref[0, 1]
    pbuf[0, 0, 0, 0:8] = jnp.full((8, TOK), first, jnp.int32)
    pbuf[0, 0, 0, 8:16] = jnp.full((8, TOK), second, jnp.int32)

    barrier = pltpu.get_barrier_semaphore()
    for device in (right, left, sibling, after, before):
        pl.semaphore_signal(barrier, inc=1, device_id=device, device_id_type=MESH)
    pl.semaphore_wait(barrier, 5)

    started = []

    def unit(kind, d, rx, side):
        if kind == POS:
            return pbuf.at[d, rx, side]
        return kvbuf.at[d, rx, side, kind]

    def send(kind, src, dst, side, sem, device):
        recv = (recv_sib if side else recv_ici).at[dst[0], dst[1], kind]
        copy = pltpu.make_async_remote_copy(
            src_ref=unit(kind, src[0], src[1], 0), dst_ref=unit(kind, dst[0], dst[1], side),
            send_sem=sem, recv_sem=recv, device_id=device, device_id_type=MESH)
        copy.start()
        started.append(copy)

    def to_sibling(d, rx, kind):
        send(kind, (d, rx), (d, rx), 1, send_sib.at[d, rx, kind], sibling)

    def to_after(d, rx, kind):
        send(kind, (d, rx), (d + 1, rx), 0, send_z.at[d, rx, kind], after)

    def to_right(d, rx, kind):
        target = 1 if rx == 0 else 3
        send(kind, (d, rx), (d, target), 0, send_x.at[d, 0, rx, kind], right)

    def to_left(d, rx, kind):
        target = 2 if rx == 0 else 3
        send(kind, (d, rx), (d, target), 0, send_x.at[d, 1, rx, kind], left)

    waited = set()

    def wait_unit(d, rx, kind, side):
        if (d, rx, kind, side) in waited or (d, rx, side) == (0, 0, 0):
            return
        waited.add((d, rx, kind, side))
        ref = unit(kind, d, rx, side)
        recv = (recv_sib if side else recv_ici).at[d, rx, kind]
        pltpu.make_async_remote_copy(
            src_ref=ref, dst_ref=ref, send_sem=local_sem.at[2, 1], recv_sem=recv,
            device_id=sibling, device_id_type=MESH).wait_recv()

    def got(d, rx, kind):
        if (d, rx, kind, 0) in waited:
            return
        wait_unit(d, rx, kind, 0)
        if rx == 0:
            if d < 2:
                to_after(d, 0, kind)
            if kind == POS:
                to_right(d, 0, POS)
                to_left(d, 0, POS)
            elif kind == H0:
                to_right(d, 0, H0)
            else:
                to_left(d, 0, H1)
                to_right(d, 0, H1)
                to_left(d, 0, H0)
        elif rx == 1 and d != 1 and kind in (POS, H0):
            to_right(d, 1, kind)
        elif rx == 2 and d != 1 and kind == H1:
            to_left(d, 2, kind)
        elif rx == 3 and d == 0:
            to_after(d, 3, kind)
        to_sibling(d, rx, kind)

    row = lax.broadcasted_iota(jnp.int32, (TOK, TOK), 0)
    col = lax.broadcasted_iota(jnp.int32, (TOK, TOK), 1)
    which = jnp.where(row // STRETCH == col, 1.0, 0.0).astype(jnp.bfloat16)
    which = jnp.concatenate([which] * (TILE // TOK), axis=0)
    eye = jnp.where(row == col, 1.0, 0.0).astype(jnp.bfloat16)

    def causal():
        later = (row // STRETCH == col // STRETCH) & (row > col)
        hide = jnp.where(later, HIDDEN, 0.0)
        return jnp.concatenate([hide] * (TILE // TOK), axis=1)

    def swapped(a, b):
        return lax.dot_general(a, b, (((1,), (1,)), ((), ())), preferred_element_type=jnp.float32)

    def attend(chunks, halves=(H0, H1), is_first=False, is_last=False):
        for d, rx in chunks:
            for kind in (POS,) + halves:
                got(d, rx, kind)
        for d, rx in chunks:
            for kind in (POS,) + halves:
                wait_unit(d, rx, kind, 1)
        pieces = [(d, rx, side) for d, rx in chunks for side in range(2)]
        num_keys = TOK * len(pieces)
        lane = lax.broadcasted_iota(jnp.int32, (8, HD), 1)
        for i, (d, rx, side) in enumerate(pieces):
            for half in range(2):
                stretch = pbuf[d, rx, side, 8 * half:8 * half + 8, :]
                seen_first = (stretch >= start_first) & (stretch <= first)
                seen_second = (stretch >= start_second) & (stretch <= second)
                seen = jnp.where(lane == 0, seen_first.astype(jnp.int32), seen_second.astype(jnp.int32))
                hide = jnp.where(seen == 1, 0.0, HIDDEN)
                at = i * TOK + half * STRETCH
                extra[at:at + STRETCH, :] = jnp.concatenate([hide] * 8, axis=0).astype(jnp.bfloat16)

        def load(half, inner):
            lanes = pl.ds(pl.multiple_of(inner * HD, HD), HD)
            keys = jnp.concatenate(
                [kvbuf[d, rx, side, half, 0, :, lanes] for d, rx, side in pieces], axis=0)
            vals = jnp.concatenate(
                [kvbuf[d, rx, side, half, 1, :, lanes] for d, rx, side in pieces], axis=0)
            keys = jnp.concatenate([keys, extra[:num_keys, :]], axis=1)
            vals = swapped(eye, vals).astype(jnp.bfloat16)
            vals = jnp.concatenate([vals, jnp.ones((SUM_ROWS, num_keys), jnp.bfloat16)], axis=0)
            return half * HALF_HEADS + inner, keys, vals

        def score(loaded, tile):
            head, keys, _ = loaded
            queries = []
            for j in range(TILE // TOK):
                group = tile * (TILE // TOK) + j
                lanes = pl.ds(pl.multiple_of((head * GROUPS + group) * HD, HD), HD)
                queries.append(q_vm[:, lanes])
            queries = jnp.concatenate([jnp.concatenate(queries, axis=0), which], axis=1)
            return swapped(keys, queries)

        def absorb(loaded, tile, scores):
            head, _, vals = loaded
            rows = slice(tile * TILE, (tile + 1) * TILE)
            if is_first:
                scores = jnp.concatenate([scores[:TOK] + causal(), scores[TOK:]], axis=0)
            scores = scores.reshape(num_keys // 8, 8, TILE)
            top = jnp.max(jnp.max(scores, axis=0), axis=0, keepdims=True) * SCALE
            top = jnp.broadcast_to(top, (8, TILE))
            if not is_first:
                old = run_max[head, :, rows]
                top = jnp.maximum(old, top)
            weights = jnp.exp2(scores * SCALE - top[None])
            weights = weights.reshape(num_keys, TILE).astype(jnp.bfloat16)
            part = lax.dot_general(
                vals, weights, (((1,), (0,)), ((), ())), preferred_element_type=jnp.float32)
            part = part.reshape(ACC_ROWS // 8, 8, TILE)
            if not is_first:
                factor = jnp.exp2(old - top)
                part = part + acc[head, :, rows].reshape(ACC_ROWS // 8, 8, TILE) * factor[None]
            if is_last:
                inverse = 1.0 / part[HD // 8]
                result = (part[:HD // 8] * inverse[None]).reshape(HD, TILE).astype(jnp.bfloat16)
                for j in range(TILE // TOK):
                    group = tile * (TILE // TOK) + j
                    place = pl.ds(pl.multiple_of((head * GROUPS + group) * HD, HD), HD)
                    turned = swapped(eye, result[:, j * TOK:(j + 1) * TOK])
                    out_vm[:, place] = turned.astype(jnp.bfloat16)
            else:
                acc[head, :, rows] = part.reshape(ACC_ROWS, TILE)
                run_max[head, :, rows] = top

        steps = HALF_HEADS // HEADS_AT_ONCE

        def some_heads(step, carry):
            half = halves[0] if len(halves) == 1 else step // steps
            work = []
            for i in range(HEADS_AT_ONCE):
                loaded = load(half, (step % steps) * HEADS_AT_ONCE + i)
                work += [(loaded, tile) for tile in range(ROWS // TILE)]
            scores = score(*work[0])
            for i, (loaded, tile) in enumerate(work):
                following = score(*work[i + 1]) if i + 1 < len(work) else None
                absorb(loaded, tile, scores)
                scores = following
            if is_last:
                output(step).start()
            return carry

        lax.fori_loop(0, steps * len(halves), some_heads, 0)

    def output(step):
        lanes = pl.ds(pl.multiple_of(step * OUT_LANES, OUT_LANES), OUT_LANES)
        return pltpu.make_async_copy(out_vm.at[:, lanes], out_hbm.at[0, :, lanes], out_sem.at[step])

    for device in (to_sibling, to_after, to_right, to_left):
        device(0, 0, POS)
    local[0].wait()
    local[1].wait()
    to_right(0, 0, H0)
    to_sibling(0, 0, H0)
    to_after(0, 0, H0)
    local[2].wait()
    local[3].wait()
    to_left(0, 0, H1)
    to_sibling(0, 0, H1)
    to_after(0, 0, H1)
    to_right(0, 0, H1)
    to_left(0, 0, H0)
    for kind in (POS, H0, H1):
        waited.add((0, 0, kind, 0))

    end = jnp.int32(0)
    start_first = jnp.int32(0)
    start_second = jnp.int32(0)
    for r in range(REQS):
        end = end + len_ref[r]
        start_first = jnp.where(end <= first, end, start_first)
        start_second = jnp.where(end <= second, end, start_second)

    queries_in.wait()
    attend([(0, 0)], is_first=True)

    got(0, 1, POS)
    got(0, 1, H0)
    got(0, 2, H1)
    got(1, 0, POS)
    got(1, 0, H0)
    attend([(0, 1)], (H0,))
    attend([(0, 2)], (H1,))
    got(1, 0, H1)
    attend([(0, 1), (1, 0)], (H1,))
    attend([(0, 2), (1, 0)], (H0,))
    for kind in (POS, H0, H1):
        got(0, 3, kind)
    got(2, 0, POS)
    got(2, 0, H0)
    attend([(0, 3)])
    got(2, 0, H1)
    attend([(2, 0), (1, 1)], (H0,))
    attend([(2, 0), (1, 2)], (H1,))
    got(1, 1, H1)
    got(1, 2, H0)
    attend([(1, 1), (1, 3)], (H1,))
    got(2, 1, POS)
    got(2, 1, H0)
    got(2, 2, H1)
    attend([(1, 2), (1, 3)], (H0,))
    attend([(2, 1), (2, 2)])
    attend([(2, 3)], is_last=True)

    for step in range(NUM_OUT):
        output(step).wait()
    for copy in started:
        copy.wait_send()


def copy_kernel(source, target, held, sems):
    parts = []
    for part in range(COPY_PARTS):
        rows = slice(part * 16, (part + 1) * 16)
        parts.append((
            pltpu.make_async_copy(source.at[0, rows], held.at[rows], sems.at[0, part]),
            pltpu.make_async_copy(held.at[rows], target.at[0, rows], sems.at[1, part])))
    for come, _ in parts:
        come.start()
    for come, leave in parts:
        come.wait()
        leave.start()
    for _, leave in parts:
        leave.wait()


def body(queries, keys, values, placement, lengths):
    any_spec = pl.BlockSpec(memory_space=pl.ANY)
    smem = pl.BlockSpec(memory_space=pltpu.SMEM)
    dma = pltpu.SemaphoreType.DMA
    out_shape = jax.ShapeDtypeStruct((1, TOK, KVH * GROUPS * HD), jnp.bfloat16)
    result = pl.pallas_call(
        kernel,
        out_shape=out_shape,
        in_specs=[any_spec, any_spec, any_spec, smem, smem],
        out_specs=any_spec,
        scratch_shapes=[
            pltpu.VMEM((3, NUM_X, 2, 2, 2, TOK, HALF_LANES), jnp.bfloat16),
            pltpu.VMEM((3, NUM_X, 2, 16, TOK), jnp.int32),
            pltpu.VMEM((TOK, KVH * GROUPS * HD), jnp.bfloat16),
            pltpu.VMEM((TOK, KVH * GROUPS * HD), jnp.bfloat16),
            pltpu.VMEM((KVH, ACC_ROWS, ROWS), jnp.float32),
            pltpu.VMEM((KVH, 8, ROWS), jnp.float32),
            pltpu.VMEM((MAX_KEYS, HD), jnp.bfloat16),
            dma((3, 2)),
            dma((NUM_OUT,)),
            dma((3, NUM_X, 3)),
            dma((3, NUM_X, 3)),
            dma((2, NUM_X, 3)),
            dma((3, 2, 3, 3)),
            dma((3, NUM_X, 3)),
        ],
        compiler_params=pltpu.CompilerParams(
            collective_id=0, has_side_effects=True, vmem_limit_bytes=56 * 1024 * 1024),
        cost_estimate=pl.CostEstimate(
            flops=4 * TOK * 64 * 3072 * HD, bytes_accessed=5 * 1024 * 1024,
            transcendentals=TOK * 64 * 3072),
    )(queries, keys, values, placement, lengths)
    return pl.pallas_call(
        copy_kernel,
        out_shape=out_shape,
        in_specs=[any_spec],
        out_specs=any_spec,
        scratch_shapes=[
            pltpu.VMEM((TOK, KVH * GROUPS * HD), jnp.bfloat16),
            dma((2, COPY_PARTS)),
        ],
        compiler_params=pltpu.CompilerParams(vmem_limit_bytes=56 * 1024 * 1024),
    )(result)


def solution(mesh):
    in_specs = (
        P("grp", "ctx", None),
        P("grp", "ctx", None),
        P("grp", "ctx", None),
        P("grp", "ctx"),
        P(),
    )
    out_specs = P("grp", "ctx", None)
    return jax.shard_map(body, mesh=mesh, in_specs=in_specs, out_specs=out_specs, check_vma=False)
```

```python
import math

import jax
import jax.numpy as jnp
from jax import lax
from jax.experimental import pallas as pl
from jax.experimental.pallas import tpu as pltpu
from jax.sharding import PartitionSpec as P

HD = 128
KVH = 8
GROUPS = 8
STRETCH = 64
TOK = 128
COL_STRETCHES = 16
REQS = 32
NUM_X = 4
NUM_GRP = 32
ROWS = GROUPS * TOK
TILE = GROUPS * STRETCH
HALF_HEADS = 4
HALF_LANES = HALF_HEADS * HD
HEADS_AT_ONCE = 2
MAX_KEYS = 512
COPY_PARTS = TOK // 16
OUT_LANES = HEADS_AT_ONCE * GROUPS * HD
NUM_OUT = KVH // HEADS_AT_ONCE

HIDDEN = -2e30
SCALE = math.log2(math.e) / math.sqrt(HD)
MESH = pl.DeviceIdType.MESH
H0, H1, POS = 0, 1, 2


def kernel(q_hbm, k_hbm, v_hbm, place_ref, len_ref, out_hbm,
           kvbuf, pbuf, q_vm, out_vm, acc, run_max, run_sum, hide,
           local_sem, out_sem, recv_ici, recv_sib, send_z, send_x, send_sib):
    ctx = lax.axis_index("ctx")
    grp = lax.axis_index("grp")
    x = ctx // 2
    core = ctx % 2
    right = (((x + 1) % NUM_X) * 2 + core, grp)
    left = (((x + NUM_X - 1) % NUM_X) * 2 + core, grp)
    sibling = (x * 2 + 1 - core, grp)
    after = (ctx, (grp + 1) % NUM_GRP)
    before = (ctx, (grp + NUM_GRP - 1) % NUM_GRP)

    local = []
    for half in range(2):
        lanes = slice(half * HALF_LANES, (half + 1) * HALF_LANES)
        for part, source in enumerate((k_hbm, v_hbm)):
            local.append(pltpu.make_async_copy(
                source.at[0, :, lanes], kvbuf.at[0, 0, 0, half, part], local_sem.at[half, part]))
    queries_in = pltpu.make_async_copy(q_hbm.at[0], q_vm, local_sem.at[2, 0])
    for copy in local + [queries_in]:
        copy.start()

    first = grp * COL_STRETCHES + place_ref[0, 0]
    second = grp * COL_STRETCHES + place_ref[0, 1]
    pbuf[0, 0, 0, 0:8] = jnp.full((8, TOK), first, jnp.int32)
    pbuf[0, 0, 0, 8:16] = jnp.full((8, TOK), second, jnp.int32)

    barrier = pltpu.get_barrier_semaphore()
    for device in (right, left, sibling, after, before):
        pl.semaphore_signal(barrier, inc=1, device_id=device, device_id_type=MESH)
    pl.semaphore_wait(barrier, 5)

    started = []

    def unit(kind, d, rx, side):
        if kind == POS:
            return pbuf.at[d, rx, side]
        return kvbuf.at[d, rx, side, kind]

    def send(kind, src, dst, side, sem, device):
        recv = (recv_sib if side else recv_ici).at[dst[0], dst[1], kind]
        copy = pltpu.make_async_remote_copy(
            src_ref=unit(kind, src[0], src[1], 0), dst_ref=unit(kind, dst[0], dst[1], side),
            send_sem=sem, recv_sem=recv, device_id=device, device_id_type=MESH)
        copy.start()
        started.append(copy)

    def to_sibling(d, rx, kind):
        send(kind, (d, rx), (d, rx), 1, send_sib.at[d, rx, kind], sibling)

    def to_after(d, rx, kind):
        send(kind, (d, rx), (d + 1, rx), 0, send_z.at[d, rx, kind], after)

    def to_right(d, rx, kind):
        target = 1 if rx == 0 else 3
        send(kind, (d, rx), (d, target), 0, send_x.at[d, 0, rx, kind], right)

    def to_left(d, rx, kind):
        target = 2 if rx == 0 else 3
        send(kind, (d, rx), (d, target), 0, send_x.at[d, 1, rx, kind], left)

    waited = set()

    def wait_unit(d, rx, kind, side):
        if (d, rx, kind, side) in waited or (d, rx, side) == (0, 0, 0):
            return
        waited.add((d, rx, kind, side))
        ref = unit(kind, d, rx, side)
        recv = (recv_sib if side else recv_ici).at[d, rx, kind]
        pltpu.make_async_remote_copy(
            src_ref=ref, dst_ref=ref, send_sem=local_sem.at[2, 1], recv_sem=recv,
            device_id=sibling, device_id_type=MESH).wait_recv()

    def got(d, rx, kind):
        if (d, rx, kind, 0) in waited:
            return
        wait_unit(d, rx, kind, 0)
        if rx == 0:
            if d < 2:
                to_after(d, 0, kind)
            if kind == POS:
                to_right(d, 0, POS)
                to_left(d, 0, POS)
            elif kind == H0:
                to_right(d, 0, H0)
            else:
                to_left(d, 0, H1)
                to_right(d, 0, H1)
                to_left(d, 0, H0)
        elif rx == 1 and d != 1 and kind in (POS, H0):
            to_right(d, 1, kind)
        elif rx == 2 and d != 1 and kind == H1:
            to_left(d, 2, kind)
        elif rx == 3 and d == 0:
            to_after(d, 3, kind)
        to_sibling(d, rx, kind)

    def causal(t):
        row = lax.broadcasted_iota(jnp.int32, (STRETCH, TOK), 0)
        col = lax.broadcasted_iota(jnp.int32, (STRETCH, TOK), 1)
        later = (col // STRETCH == t) & (col % STRETCH > row)
        return jnp.where(later, HIDDEN, 0.0)

    def swapped(a, b):
        return lax.dot_general(a, b, (((1,), (1,)), ((), ())), preferred_element_type=jnp.float32)

    def attend(chunks, halves=(H0, H1), is_first=False, is_last=False):
        for d, rx in chunks:
            for kind in (POS,) + halves:
                got(d, rx, kind)
        for d, rx in chunks:
            for kind in (POS,) + halves:
                wait_unit(d, rx, kind, 1)
        pieces = [(d, rx, side) for d, rx in chunks for side in range(2)]
        num_keys = TOK * len(pieces)
        lane = lax.broadcasted_iota(jnp.int32, (8, TOK), 1)
        for i, (d, rx, side) in enumerate(pieces):
            stretch = jnp.where(lane < STRETCH, pbuf[d, rx, side, 0:8, :], pbuf[d, rx, side, 8:16, :])
            for t, (low, high) in enumerate(((start_first, first), (start_second, second))):
                seen = (stretch >= low) & (stretch <= high)
                hide[t, :, i * TOK:(i + 1) * TOK] = jnp.where(seen, 0.0, HIDDEN)

        def load(half, inner):
            lanes = pl.ds(pl.multiple_of(inner * HD, HD), HD)
            keys = jnp.concatenate(
                [kvbuf[d, rx, side, half, 0, :, lanes] for d, rx, side in pieces], axis=0)
            vals = jnp.concatenate(
                [kvbuf[d, rx, side, half, 1, :, lanes] for d, rx, side in pieces], axis=0)
            return half * HALF_HEADS + inner, keys, vals

        def score(loaded):
            head, keys, _ = loaded
            queries = []
            for t in range(2):
                for group in range(GROUPS):
                    lanes = pl.ds(pl.multiple_of((head * GROUPS + group) * HD, HD), HD)
                    queries.append(q_vm[t * STRETCH:(t + 1) * STRETCH, lanes])
            return swapped(jnp.concatenate(queries, axis=0), keys)

        def absorb(loaded, scores):
            head, _, vals = loaded
            masked = []
            for t in range(2):
                part = scores[t * TILE:(t + 1) * TILE]
                if is_first:
                    own = part[:, :TOK].reshape(GROUPS, STRETCH, TOK) + causal(t)[None]
                    part = jnp.concatenate([own.reshape(TILE, TOK), part[:, TOK:]], axis=1)
                part = part.reshape(TILE // 8, 8, num_keys) + hide[t, :, :num_keys][None]
                masked.append(part.reshape(TILE, num_keys))
            masked = jnp.concatenate(masked, axis=0)
            top = jnp.broadcast_to(jnp.max(masked, axis=1, keepdims=True), (ROWS, HD)) * SCALE
            if not is_first:
                old = run_max[head]
                top = jnp.maximum(old, top)
            tops = jnp.concatenate([top] * (num_keys // HD), axis=1)
            weights = jnp.exp2(masked * SCALE - tops)
            total = weights[:, :HD]
            for j in range(1, num_keys // HD):
                total = total + weights[:, j * HD:(j + 1) * HD]
            part = lax.dot_general(
                weights.astype(jnp.bfloat16), vals, (((1,), (0,)), ((), ())),
                preferred_element_type=jnp.float32)
            if not is_first:
                factor = jnp.exp2(old - top)
                part = part + acc[head] * factor
                total = total + run_sum[head] * factor
            if is_last:
                result = (part / jnp.sum(total, axis=1, keepdims=True)).astype(jnp.bfloat16)
                for t in range(2):
                    for group in range(GROUPS):
                        place = pl.ds(pl.multiple_of((head * GROUPS + group) * HD, HD), HD)
                        at = (t * GROUPS + group) * STRETCH
                        out_vm[t * STRETCH:(t + 1) * STRETCH, place] = result[at:at + STRETCH]
            else:
                acc[head] = part
                run_sum[head] = total
                run_max[head] = top

        steps = HALF_HEADS // HEADS_AT_ONCE

        def some_heads(step, carry):
            half = halves[0] if len(halves) == 1 else step // steps
            work = [load(half, (step % steps) * HEADS_AT_ONCE + i) for i in range(HEADS_AT_ONCE)]
            scores = score(work[0])
            for i, loaded in enumerate(work):
                following = score(work[i + 1]) if i + 1 < len(work) else None
                absorb(loaded, scores)
                scores = following
            if is_last:
                output(step).start()
            return carry

        lax.fori_loop(0, steps * len(halves), some_heads, 0)

    def output(step):
        lanes = pl.ds(pl.multiple_of(step * OUT_LANES, OUT_LANES), OUT_LANES)
        return pltpu.make_async_copy(out_vm.at[:, lanes], out_hbm.at[0, :, lanes], out_sem.at[step])

    for device in (to_sibling, to_after, to_right, to_left):
        device(0, 0, POS)
    local[0].wait()
    local[1].wait()
    to_right(0, 0, H0)
    to_sibling(0, 0, H0)
    to_after(0, 0, H0)
    local[2].wait()
    local[3].wait()
    to_left(0, 0, H1)
    to_sibling(0, 0, H1)
    to_after(0, 0, H1)
    to_right(0, 0, H1)
    to_left(0, 0, H0)
    for kind in (POS, H0, H1):
        waited.add((0, 0, kind, 0))

    end = jnp.int32(0)
    start_first = jnp.int32(0)
    start_second = jnp.int32(0)
    for r in range(REQS):
        end = end + len_ref[r]
        start_first = jnp.where(end <= first, end, start_first)
        start_second = jnp.where(end <= second, end, start_second)

    queries_in.wait()
    attend([(0, 0)], is_first=True)

    got(0, 1, POS)
    got(0, 1, H0)
    got(0, 2, H1)
    got(1, 0, POS)
    got(1, 0, H0)
    attend([(0, 1)], (H0,))
    attend([(0, 2)], (H1,))
    got(1, 0, H1)
    attend([(0, 1), (1, 0)], (H1,))
    attend([(0, 2), (1, 0)], (H0,))
    for kind in (POS, H0, H1):
        got(0, 3, kind)
    got(2, 0, POS)
    got(2, 0, H0)
    attend([(0, 3)])
    got(2, 0, H1)
    attend([(2, 0), (1, 1)], (H0,))
    attend([(2, 0), (1, 2)], (H1,))
    got(1, 1, H1)
    got(1, 2, H0)
    attend([(1, 1), (1, 3)], (H1,))
    got(2, 1, POS)
    got(2, 1, H0)
    got(2, 2, H1)
    attend([(1, 2), (1, 3)], (H0,))
    attend([(2, 1), (2, 2)])
    attend([(2, 3)], is_last=True)

    for step in range(NUM_OUT):
        output(step).wait()
    for copy in started:
        copy.wait_send()


def copy_kernel(source, target, held, sems):
    parts = []
    for part in range(COPY_PARTS):
        rows = slice(part * 16, (part + 1) * 16)
        parts.append((
            pltpu.make_async_copy(source.at[0, rows], held.at[rows], sems.at[0, part]),
            pltpu.make_async_copy(held.at[rows], target.at[0, rows], sems.at[1, part])))
    for come, _ in parts:
        come.start()
    for come, leave in parts:
        come.wait()
        leave.start()
    for _, leave in parts:
        leave.wait()


def body(queries, keys, values, placement, lengths):
    any_spec = pl.BlockSpec(memory_space=pl.ANY)
    smem = pl.BlockSpec(memory_space=pltpu.SMEM)
    dma = pltpu.SemaphoreType.DMA
    out_shape = jax.ShapeDtypeStruct((1, TOK, KVH * GROUPS * HD), jnp.bfloat16)
    result = pl.pallas_call(
        kernel,
        out_shape=out_shape,
        in_specs=[any_spec, any_spec, any_spec, smem, smem],
        out_specs=any_spec,
        scratch_shapes=[
            pltpu.VMEM((3, NUM_X, 2, 2, 2, TOK, HALF_LANES), jnp.bfloat16),
            pltpu.VMEM((3, NUM_X, 2, 16, TOK), jnp.int32),
            pltpu.VMEM((TOK, KVH * GROUPS * HD), jnp.bfloat16),
            pltpu.VMEM((TOK, KVH * GROUPS * HD), jnp.bfloat16),
            pltpu.VMEM((KVH, ROWS, HD), jnp.float32),
            pltpu.VMEM((KVH, ROWS, HD), jnp.float32),
            pltpu.VMEM((KVH, ROWS, HD), jnp.float32),
            pltpu.VMEM((2, 8, MAX_KEYS), jnp.float32),
            dma((3, 2)),
            dma((NUM_OUT,)),
            dma((3, NUM_X, 3)),
            dma((3, NUM_X, 3)),
            dma((2, NUM_X, 3)),
            dma((3, 2, 3, 3)),
            dma((3, NUM_X, 3)),
        ],
        compiler_params=pltpu.CompilerParams(
            collective_id=0, has_side_effects=True, vmem_limit_bytes=56 * 1024 * 1024),
        cost_estimate=pl.CostEstimate(
            flops=4 * TOK * 64 * 3072 * HD, bytes_accessed=5 * 1024 * 1024,
            transcendentals=TOK * 64 * 3072),
    )(queries, keys, values, placement, lengths)
    return pl.pallas_call(
        copy_kernel,
        out_shape=out_shape,
        in_specs=[any_spec],
        out_specs=any_spec,
        scratch_shapes=[
            pltpu.VMEM((TOK, KVH * GROUPS * HD), jnp.bfloat16),
            dma((2, COPY_PARTS)),
        ],
        compiler_params=pltpu.CompilerParams(vmem_limit_bytes=56 * 1024 * 1024),
    )(result)


def solution(mesh):
    in_specs = (
        P("grp", "ctx", None),
        P("grp", "ctx", None),
        P("grp", "ctx", None),
        P("grp", "ctx"),
        P(),
    )
    out_specs = P("grp", "ctx", None)
    return jax.shard_map(body, mesh=mesh, in_specs=in_specs, out_specs=out_specs, check_vma=False)
```

```python
import math

import jax
import jax.numpy as jnp
from jax import lax
from jax.experimental import pallas as pl
from jax.experimental.pallas import tpu as pltpu
from jax.sharding import PartitionSpec as P

HD = 128
KVH = 8
GROUPS = 8
STRETCH = 64
TOK = 128
COL_STRETCHES = 16
REQS = 32
NUM_X = 4
NUM_GRP = 32
ROWS = GROUPS * TOK
TILE = 512
HALF_HEADS = 4
HALF_LANES = HALF_HEADS * HD
HEADS_AT_ONCE = 2
MAX_KEYS = 512
COPY_PARTS = TOK // 16
BLOCK = 32
OUT_LANES = HEADS_AT_ONCE * GROUPS * HD
NUM_OUT = KVH // HEADS_AT_ONCE

HIDDEN = -2e30
SCALE = math.log2(math.e) / math.sqrt(HD)
MESH = pl.DeviceIdType.MESH
H0, H1, POS = 0, 1, 2


def kernel(q_hbm, k_hbm, v_hbm, place_ref, len_ref, out_hbm,
           kvbuf, pbuf, q_vm, out_vm, acc, run_max, extra, s_buf, p_buf, f_buf,
           local_sem, out_sem, recv_ici, recv_sib, send_z, send_x, send_sib):
    ctx = lax.axis_index("ctx")
    grp = lax.axis_index("grp")
    x = ctx // 2
    core = ctx % 2
    right = (((x + 1) % NUM_X) * 2 + core, grp)
    left = (((x + NUM_X - 1) % NUM_X) * 2 + core, grp)
    sibling = (x * 2 + 1 - core, grp)
    after = (ctx, (grp + 1) % NUM_GRP)
    before = (ctx, (grp + NUM_GRP - 1) % NUM_GRP)

    local = []
    for half in range(2):
        lanes = slice(half * HALF_LANES, (half + 1) * HALF_LANES)
        for part, source in enumerate((k_hbm, v_hbm)):
            local.append(pltpu.make_async_copy(
                source.at[0, :, lanes], kvbuf.at[0, 0, 0, half, part], local_sem.at[half, part]))
    queries_in = pltpu.make_async_copy(q_hbm.at[0], q_vm, local_sem.at[2, 0])
    for copy in local + [queries_in]:
        copy.start()

    first = grp * COL_STRETCHES + place_ref[0, 0]
    second = grp * COL_STRETCHES + place_ref[0, 1]
    pbuf[0, 0, 0, 0:8] = jnp.full((8, TOK), first, jnp.int32)
    pbuf[0, 0, 0, 8:16] = jnp.full((8, TOK), second, jnp.int32)

    barrier = pltpu.get_barrier_semaphore()
    for device in (right, left, sibling, after, before):
        pl.semaphore_signal(barrier, inc=1, device_id=device, device_id_type=MESH)
    pl.semaphore_wait(barrier, 5)

    started = []

    def unit(kind, d, rx, side):
        if kind == POS:
            return pbuf.at[d, rx, side]
        return kvbuf.at[d, rx, side, kind]

    def send(kind, src, dst, side, sem, device):
        recv = (recv_sib if side else recv_ici).at[dst[0], dst[1], kind]
        copy = pltpu.make_async_remote_copy(
            src_ref=unit(kind, src[0], src[1], 0), dst_ref=unit(kind, dst[0], dst[1], side),
            send_sem=sem, recv_sem=recv, device_id=device, device_id_type=MESH)
        copy.start()
        started.append(copy)

    def to_sibling(d, rx, kind):
        send(kind, (d, rx), (d, rx), 1, send_sib.at[d, rx, kind], sibling)

    def to_after(d, rx, kind):
        send(kind, (d, rx), (d + 1, rx), 0, send_z.at[d, rx, kind], after)

    def to_right(d, rx, kind):
        target = 1 if rx == 0 else 3
        send(kind, (d, rx), (d, target), 0, send_x.at[d, 0, rx, kind], right)

    def to_left(d, rx, kind):
        target = 2 if rx == 0 else 3
        send(kind, (d, rx), (d, target), 0, send_x.at[d, 1, rx, kind], left)

    waited = set()

    def wait_unit(d, rx, kind, side):
        if (d, rx, kind, side) in waited or (d, rx, side) == (0, 0, 0):
            return
        waited.add((d, rx, kind, side))
        ref = unit(kind, d, rx, side)
        recv = (recv_sib if side else recv_ici).at[d, rx, kind]
        pltpu.make_async_remote_copy(
            src_ref=ref, dst_ref=ref, send_sem=local_sem.at[2, 1], recv_sem=recv,
            device_id=sibling, device_id_type=MESH).wait_recv()

    def got(d, rx, kind):
        if (d, rx, kind, 0) in waited:
            return
        wait_unit(d, rx, kind, 0)
        if rx == 0:
            if d < 2:
                to_after(d, 0, kind)
            if kind == POS:
                to_right(d, 0, POS)
                to_left(d, 0, POS)
            elif kind == H0:
                to_right(d, 0, H0)
            else:
                to_left(d, 0, H1)
                to_right(d, 0, H1)
                to_left(d, 0, H0)
        elif rx == 1 and d != 1 and kind in (POS, H0):
            to_right(d, 1, kind)
        elif rx == 2 and d != 1 and kind == H1:
            to_left(d, 2, kind)
        elif rx == 3 and d == 0:
            to_after(d, 3, kind)
        to_sibling(d, rx, kind)

    def causal(start):
        row = lax.broadcasted_iota(jnp.int32, (BLOCK, TOK), 0) + start
        col = lax.broadcasted_iota(jnp.int32, (BLOCK, TOK), 1)
        later = (row // STRETCH == col // STRETCH) & (col > row)
        return jnp.where(later, HIDDEN, 0.0)

    row = lax.broadcasted_iota(jnp.int32, (TOK, HD), 0)
    col = lax.broadcasted_iota(jnp.int32, (TOK, HD), 1)
    which = jnp.where(row // STRETCH == col, 1.0, 0.0).astype(jnp.bfloat16)
    which = jnp.concatenate([which] * (TILE // TOK), axis=0)

    def attend(chunks, halves=(H0, H1), is_first=False, is_last=False):
        for d, rx in chunks:
            for kind in (POS,) + halves:
                got(d, rx, kind)
        for d, rx in chunks:
            for kind in (POS,) + halves:
                wait_unit(d, rx, kind, 1)
        pieces = [(d, rx, side) for d, rx in chunks for side in range(2)]
        num_keys = TOK * len(pieces)
        lane = lax.broadcasted_iota(jnp.int32, (8, HD), 1)
        for i, (d, rx, side) in enumerate(pieces):
            for half in range(2):
                stretch = pbuf[d, rx, side, 8 * half:8 * half + 8, :]
                seen_first = (stretch >= start_first) & (stretch <= first)
                seen_second = (stretch >= start_second) & (stretch <= second)
                seen = jnp.where(lane == 0, seen_first.astype(jnp.int32), seen_second.astype(jnp.int32))
                hide = jnp.where(seen == 1, 0.0, HIDDEN)
                at = i * TOK + half * STRETCH
                extra[at:at + STRETCH, :] = jnp.concatenate([hide] * 8, axis=0).astype(jnp.bfloat16)

        def load(half, inner):
            lanes = pl.ds(pl.multiple_of(inner * HD, HD), HD)
            keys = jnp.concatenate(
                [kvbuf[d, rx, side, half, 0, :, lanes] for d, rx, side in pieces], axis=0)
            vals = jnp.concatenate(
                [kvbuf[d, rx, side, half, 1, :, lanes] for d, rx, side in pieces], axis=0)
            keys = jnp.concatenate([keys, extra[:num_keys, :]], axis=1)
            vals = jnp.concatenate([vals, jnp.ones_like(vals)], axis=1)
            return half * HALF_HEADS + inner, keys, vals

        def score(loaded, tile):
            head, keys, _ = loaded
            queries = []
            for j in range(TILE // TOK):
                group = tile * (TILE // TOK) + j
                lanes = pl.ds(pl.multiple_of((head * GROUPS + group) * HD, HD), HD)
                queries.append(q_vm[:, lanes])
            queries = jnp.concatenate([jnp.concatenate(queries, axis=0), which], axis=1)
            return lax.dot_general(
                queries, keys, (((1,), (1,)), ((), ())), preferred_element_type=jnp.float32)

        def absorb(loaded, tile, slot):
            head, _, vals = loaded
            first_row = tile * TILE
            for at in range(0, TILE, BLOCK):
                rows = slice(first_row + at, first_row + at + BLOCK)
                block = s_buf[slot, at:at + BLOCK, :num_keys]
                if is_first:
                    own = block[:, :TOK] + causal(at % TOK)
                    s_buf[slot, at:at + BLOCK, :TOK] = own
                    block = jnp.concatenate([own, block[:, TOK:]], axis=1)
                top = jnp.broadcast_to(jnp.max(block, axis=1, keepdims=True), (BLOCK, HD)) * SCALE
                if not is_first:
                    old = run_max[head, rows]
                    top = jnp.maximum(old, top)
                    f_buf[slot, at:at + BLOCK] = jnp.exp2(old - top)
                run_max[head, rows] = top
            for at in range(0, TILE, BLOCK):
                top = run_max[head, first_row + at:first_row + at + BLOCK]
                for j in range(0, num_keys, HD):
                    weights = jnp.exp2(s_buf[slot, at:at + BLOCK, j:j + HD] * SCALE - top)
                    p_buf[slot, at:at + BLOCK, j:j + HD] = weights.astype(jnp.bfloat16)
            part = lax.dot_general(
                p_buf[slot, :, :num_keys], vals, (((1,), (0,)), ((), ())),
                preferred_element_type=jnp.float32)
            for at in range(0, TILE, BLOCK):
                rows = slice(first_row + at, first_row + at + BLOCK)
                block = part[at:at + BLOCK]
                if not is_first:
                    factor = f_buf[slot, at:at + BLOCK]
                    block = block + acc[head, rows] * jnp.concatenate([factor, factor], axis=1)
                if is_last:
                    group = (first_row + at) // TOK
                    place = pl.ds(pl.multiple_of((head * GROUPS + group) * HD, HD), HD)
                    result = (block[:, :HD] / block[:, HD:]).astype(jnp.bfloat16)
                    out_vm[at % TOK:at % TOK + BLOCK, place] = result
                else:
                    acc[head, rows] = block

        steps = HALF_HEADS // HEADS_AT_ONCE

        def some_heads(step, carry):
            half = halves[0] if len(halves) == 1 else step // steps
            work = []
            for i in range(HEADS_AT_ONCE):
                loaded = load(half, (step % steps) * HEADS_AT_ONCE + i)
                work += [(loaded, tile) for tile in range(ROWS // TILE)]
            s_buf[0, :, :num_keys] = score(*work[0])
            for i, (loaded, tile) in enumerate(work):
                if i + 1 < len(work):
                    s_buf[(i + 1) % 2, :, :num_keys] = score(*work[i + 1])
                absorb(loaded, tile, i % 2)
            if is_last:
                output(step).start()
            return carry

        lax.fori_loop(0, steps * len(halves), some_heads, 0)

    def output(step):
        lanes = pl.ds(pl.multiple_of(step * OUT_LANES, OUT_LANES), OUT_LANES)
        return pltpu.make_async_copy(out_vm.at[:, lanes], out_hbm.at[0, :, lanes], out_sem.at[step])

    for device in (to_sibling, to_after, to_right, to_left):
        device(0, 0, POS)
    local[0].wait()
    local[1].wait()
    to_right(0, 0, H0)
    to_sibling(0, 0, H0)
    to_after(0, 0, H0)
    local[2].wait()
    local[3].wait()
    to_left(0, 0, H1)
    to_sibling(0, 0, H1)
    to_after(0, 0, H1)
    to_right(0, 0, H1)
    to_left(0, 0, H0)
    for kind in (POS, H0, H1):
        waited.add((0, 0, kind, 0))

    end = jnp.int32(0)
    start_first = jnp.int32(0)
    start_second = jnp.int32(0)
    for r in range(REQS):
        end = end + len_ref[r]
        start_first = jnp.where(end <= first, end, start_first)
        start_second = jnp.where(end <= second, end, start_second)

    queries_in.wait()
    attend([(0, 0)], is_first=True)

    got(0, 1, POS)
    got(0, 1, H0)
    got(0, 2, H1)
    got(1, 0, POS)
    got(1, 0, H0)
    attend([(0, 1)], (H0,))
    attend([(0, 2)], (H1,))
    got(1, 0, H1)
    attend([(0, 1), (1, 0)], (H1,))
    attend([(0, 2), (1, 0)], (H0,))
    for kind in (POS, H0, H1):
        got(0, 3, kind)
    got(2, 0, POS)
    got(2, 0, H0)
    attend([(0, 3)])
    got(2, 0, H1)
    attend([(2, 0), (1, 1)], (H0,))
    attend([(2, 0), (1, 2)], (H1,))
    got(1, 1, H1)
    got(1, 2, H0)
    attend([(1, 1), (1, 3)], (H1,))
    got(2, 1, POS)
    got(2, 1, H0)
    got(2, 2, H1)
    attend([(1, 2), (1, 3)], (H0,))
    attend([(2, 1), (2, 2)])
    attend([(2, 3)], is_last=True)

    for step in range(NUM_OUT):
        output(step).wait()
    for copy in started:
        copy.wait_send()


def copy_kernel(source, target, held, sems):
    parts = []
    for part in range(COPY_PARTS):
        rows = slice(part * 16, (part + 1) * 16)
        parts.append((
            pltpu.make_async_copy(source.at[0, rows], held.at[rows], sems.at[0, part]),
            pltpu.make_async_copy(held.at[rows], target.at[0, rows], sems.at[1, part])))
    for come, _ in parts:
        come.start()
    for come, leave in parts:
        come.wait()
        leave.start()
    for _, leave in parts:
        leave.wait()


def body(queries, keys, values, placement, lengths):
    any_spec = pl.BlockSpec(memory_space=pl.ANY)
    smem = pl.BlockSpec(memory_space=pltpu.SMEM)
    dma = pltpu.SemaphoreType.DMA
    out_shape = jax.ShapeDtypeStruct((1, TOK, KVH * GROUPS * HD), jnp.bfloat16)
    result = pl.pallas_call(
        kernel,
        out_shape=out_shape,
        in_specs=[any_spec, any_spec, any_spec, smem, smem],
        out_specs=any_spec,
        scratch_shapes=[
            pltpu.VMEM((3, NUM_X, 2, 2, 2, TOK, HALF_LANES), jnp.bfloat16),
            pltpu.VMEM((3, NUM_X, 2, 16, TOK), jnp.int32),
            pltpu.VMEM((TOK, KVH * GROUPS * HD), jnp.bfloat16),
            pltpu.VMEM((TOK, KVH * GROUPS * HD), jnp.bfloat16),
            pltpu.VMEM((KVH, ROWS, 2 * HD), jnp.float32),
            pltpu.VMEM((KVH, ROWS, HD), jnp.float32),
            pltpu.VMEM((MAX_KEYS, HD), jnp.bfloat16),
            pltpu.VMEM((2, TILE, MAX_KEYS), jnp.float32),
            pltpu.VMEM((2, TILE, MAX_KEYS), jnp.bfloat16),
            pltpu.VMEM((2, TILE, HD), jnp.float32),
            dma((3, 2)),
            dma((NUM_OUT,)),
            dma((3, NUM_X, 3)),
            dma((3, NUM_X, 3)),
            dma((2, NUM_X, 3)),
            dma((3, 2, 3, 3)),
            dma((3, NUM_X, 3)),
        ],
        compiler_params=pltpu.CompilerParams(
            collective_id=0, has_side_effects=True, vmem_limit_bytes=56 * 1024 * 1024),
        cost_estimate=pl.CostEstimate(
            flops=4 * TOK * 64 * 3072 * HD, bytes_accessed=5 * 1024 * 1024,
            transcendentals=TOK * 64 * 3072),
    )(queries, keys, values, placement, lengths)
    return pl.pallas_call(
        copy_kernel,
        out_shape=out_shape,
        in_specs=[any_spec],
        out_specs=any_spec,
        scratch_shapes=[
            pltpu.VMEM((TOK, KVH * GROUPS * HD), jnp.bfloat16),
            dma((2, COPY_PARTS)),
        ],
        compiler_params=pltpu.CompilerParams(vmem_limit_bytes=56 * 1024 * 1024),
    )(result)


def solution(mesh):
    in_specs = (
        P("grp", "ctx", None),
        P("grp", "ctx", None),
        P("grp", "ctx", None),
        P("grp", "ctx"),
        P(),
    )
    out_specs = P("grp", "ctx", None)
    return jax.shard_map(body, mesh=mesh, in_specs=in_specs, out_specs=out_specs, check_vma=False)
```

```python
import math

import jax
import jax.numpy as jnp
from jax import lax
from jax.experimental import pallas as pl
from jax.experimental.pallas import tpu as pltpu
from jax.sharding import PartitionSpec as P

HD = 128
KVH = 8
GROUPS = 8
STRETCH = 64
TOK = 128
COL_STRETCHES = 16
REQS = 32
NUM_X = 4
NUM_GRP = 32
ROWS = GROUPS * TOK
TILE = 512
CORE_HEADS = KVH // 2
HALF_HEADS = CORE_HEADS // 2
HALF_LANES = HALF_HEADS * HD
CORE_LANES = CORE_HEADS * HD
HALF_OUT = HALF_HEADS * GROUPS * HD
CORE_OUT = CORE_HEADS * GROUPS * HD
CHIP_TOK = 2 * TOK
MAX_KEYS = 512
COPY_PARTS = TOK // 16

HIDDEN = -2e30
SCALE = math.log2(math.e) / math.sqrt(HD)
MESH = pl.DeviceIdType.MESH
H0, H1, POS = 0, 1, 2


def kernel(q_hbm, k_hbm, v_hbm, place_ref, len_ref, out_hbm,
           kvbuf, pbuf, q_vm, out_vm, acc, run_max, extra, which,
           local_sem, swap_send, swap_recv, out_sem, recv_ici, send_z, send_x):
    ctx = lax.axis_index("ctx")
    grp = lax.axis_index("grp")
    x = ctx // 2
    core = ctx % 2
    right = (((x + 1) % NUM_X) * 2 + core, grp)
    left = (((x + NUM_X - 1) % NUM_X) * 2 + core, grp)
    sibling = (x * 2 + 1 - core, grp)
    after = (ctx, (grp + 1) % NUM_GRP)
    before = (ctx, (grp + NUM_GRP - 1) % NUM_GRP)

    def lanes_of(which_core, half, core_lanes, half_lanes):
        start = which_core * core_lanes + half * half_lanes
        return pl.ds(pl.multiple_of(start, half_lanes), half_lanes)

    local = []
    for half in range(2):
        for part, source in enumerate((k_hbm, v_hbm)):
            local.append(pltpu.make_async_copy(
                source.at[0, :, lanes_of(core, half, CORE_LANES, HALF_LANES)],
                kvbuf.at[0, 0, half, part, 0:TOK], local_sem.at[half, part]))
    queries_in = []
    for half in range(2):
        queries_in.append(pltpu.make_async_copy(
            q_hbm.at[0, :, lanes_of(core, half, CORE_OUT, HALF_OUT)],
            q_vm.at[0, :, half * HALF_OUT:(half + 1) * HALF_OUT], local_sem.at[2, half]))
    for copy in local + queries_in:
        copy.start()

    for slot in range(2):
        pbuf[0, 0, 8 * slot:8 * slot + 8] = jnp.full(
            (8, TOK), grp * COL_STRETCHES + place_ref[0, slot], jnp.int32)

    barrier = pltpu.get_barrier_semaphore()
    for device in (right, left, sibling, after, before):
        pl.semaphore_signal(barrier, inc=1, device_id=device, device_id_type=MESH)
    pl.semaphore_wait(barrier, 5)

    started = []

    def remote(src, dst, send_sem, recv_sem, device):
        return pltpu.make_async_remote_copy(
            src_ref=src, dst_ref=dst, send_sem=send_sem, recv_sem=recv_sem,
            device_id=device, device_id_type=MESH)

    swaps = [remote(pbuf.at[0, 0, 0:16], pbuf.at[0, 0, 16:32], swap_send.at[0], swap_recv.at[0], sibling)]
    for half in range(2):
        for part, source in enumerate((k_hbm, v_hbm)):
            i = 1 + 2 * half + part
            swaps.append(remote(
                source.at[0, :, lanes_of(1 - core, half, CORE_LANES, HALF_LANES)],
                kvbuf.at[0, 0, half, part, TOK:CHIP_TOK], swap_send.at[i], swap_recv.at[i], sibling))
    for half in range(2):
        swaps.append(remote(
            q_hbm.at[0, :, lanes_of(1 - core, half, CORE_OUT, HALF_OUT)],
            q_vm.at[1, :, half * HALF_OUT:(half + 1) * HALF_OUT],
            swap_send.at[5 + half], swap_recv.at[5 + half], sibling))
    for swap in swaps[:5]:
        swap.start()

    def unit(kind, d, rx):
        if kind == POS:
            return pbuf.at[d, rx]
        return kvbuf.at[d, rx, kind]

    def send(kind, src, dst, sem, device):
        copy = remote(unit(kind, *src), unit(kind, *dst), sem, recv_ici.at[dst[0], dst[1], kind], device)
        copy.start()
        started.append(copy)

    def to_after(d, rx, kind):
        send(kind, (d, rx), (d + 1, rx), send_z.at[d, rx, kind], after)

    def to_right(d, rx, kind):
        send(kind, (d, rx), (d, 1 if rx == 0 else 3), send_x.at[d, 0, rx, kind], right)

    def to_left(d, rx, kind):
        send(kind, (d, rx), (d, 2 if rx == 0 else 3), send_x.at[d, 1, rx, kind], left)

    waited = set()

    def got(d, rx, kind):
        if (d, rx, kind) in waited:
            return
        waited.add((d, rx, kind))
        if (d, rx) != (0, 0):
            ref = unit(kind, d, rx)
            remote(ref, ref, local_sem.at[3, 0], recv_ici.at[d, rx, kind], sibling).wait_recv()
        if rx == 0:
            if kind == POS:
                to_right(d, 0, POS)
                to_left(d, 0, POS)
            elif kind == H0:
                to_right(d, 0, H0)
            else:
                to_left(d, 0, H1)
            if d < 2:
                to_after(d, 0, kind)
            if kind == H1:
                to_right(d, 0, H1)
                to_left(d, 0, H0)
        elif rx == 1 and d != 1 and kind in (POS, H0):
            to_right(d, 1, kind)
        elif rx == 2 and d != 1 and kind == H1:
            to_left(d, 2, kind)
        elif rx == 3 and d == 0:
            to_after(d, 3, kind)

    swaps[0].wait_recv()
    got(0, 0, POS)
    for half in range(2):
        for part in range(2):
            local[2 * half + part].wait()
            swaps[1 + 2 * half + part].wait_recv()
        got(0, 0, half)
    for swap in swaps[5:]:
        swap.start()

    lane = lax.broadcasted_iota(jnp.int32, (8, TOK), 1)
    highs = jnp.full((8, TOK), -1, jnp.int32)
    for t in range(4):
        highs = jnp.where(lane == t, pbuf[0, 0, 8 * t:8 * t + 8, :], highs)
    lows = jnp.zeros((8, TOK), jnp.int32)
    end = jnp.int32(0)
    for r in range(REQS):
        end = end + len_ref[r]
        lows = jnp.where(end <= highs, end, lows)

    token = lax.broadcasted_iota(jnp.int32, (TILE, HD), 0) % TOK
    column = lax.broadcasted_iota(jnp.int32, (TILE, HD), 1)
    for side in range(2):
        which[side] = jnp.where(token // STRETCH + 2 * side == column, 1.0, 0.0).astype(jnp.bfloat16)

    def causal():
        row = lax.broadcasted_iota(jnp.int32, (TOK, TOK), 0)
        col = lax.broadcasted_iota(jnp.int32, (TOK, TOK), 1)
        later = (row // STRETCH == col // STRETCH) & (col > row)
        return jnp.where(later, HIDDEN, 0.0)

    def attend(chunks, halves=(H0, H1), sides=(0, 1), is_first=False, is_last=False):
        for d, rx in chunks:
            for kind in (POS,) + halves:
                got(d, rx, kind)
        num_keys = CHIP_TOK * len(chunks)
        for i, (d, rx) in enumerate(chunks):
            for t in range(4):
                stretch = pbuf[d, rx, 8 * t:8 * t + 8, :]
                hide = jnp.where((stretch >= lows) & (stretch <= highs), 0.0, HIDDEN)
                at = i * CHIP_TOK + t * STRETCH
                extra[at:at + STRETCH, :] = jnp.concatenate([hide] * 8, axis=0).astype(jnp.bfloat16)

        def load(half, inner):
            lanes = slice(inner * HD, (inner + 1) * HD)
            keys = jnp.concatenate([kvbuf[d, rx, half, 0, :, lanes] for d, rx in chunks], axis=0)
            vals = jnp.concatenate([kvbuf[d, rx, half, 1, :, lanes] for d, rx in chunks], axis=0)
            keys = jnp.concatenate([keys, extra[:num_keys, :]], axis=1)
            vals = jnp.concatenate([vals, jnp.ones_like(vals)], axis=1)
            return half * HALF_HEADS + inner, keys, vals

        def score(loaded, side, tile):
            head, keys, _ = loaded
            queries = []
            for j in range(TILE // TOK):
                group = tile * (TILE // TOK) + j
                lanes = pl.ds(pl.multiple_of((head * GROUPS + group) * HD, HD), HD)
                queries.append(q_vm[side, :, lanes])
            queries = jnp.concatenate([jnp.concatenate(queries, axis=0), which[side]], axis=1)
            return lax.dot_general(
                queries, keys, (((1,), (1,)), ((), ())), preferred_element_type=jnp.float32)

        def absorb(loaded, side, tile, scores):
            head, _, vals = loaded
            rows = slice(tile * TILE, (tile + 1) * TILE)
            if is_first:
                own = scores[:, side * TOK:(side + 1) * TOK]
                own = (own.reshape(TILE // TOK, TOK, TOK) + causal()[None]).reshape(TILE, TOK)
                both = (own, scores[:, TOK:]) if side == 0 else (scores[:, :TOK], own)
                scores = jnp.concatenate(both, axis=1)
            top = jnp.broadcast_to(jnp.max(scores, axis=1, keepdims=True), (TILE, HD)) * SCALE
            if not is_first:
                old = run_max[head, side, rows]
                top = jnp.maximum(old, top)
            tops = jnp.concatenate([top] * (num_keys // HD), axis=1)
            weights = jnp.exp2(scores * SCALE - tops).astype(jnp.bfloat16)
            part = lax.dot_general(
                weights, vals, (((1,), (0,)), ((), ())),
                preferred_element_type=jnp.float32)
            if not is_first:
                factor = jnp.exp2(old - top)
                part = part + acc[head, side, rows] * jnp.concatenate([factor, factor], axis=1)
            if is_last:
                result = (part[:, :HD] / part[:, HD:]).astype(jnp.bfloat16)
                for j in range(TILE // TOK):
                    group = tile * (TILE // TOK) + j
                    place = pl.ds(pl.multiple_of((head * GROUPS + group) * HD, HD), HD)
                    out_vm[side, :, place] = result[j * TOK:(j + 1) * TOK]
            else:
                acc[head, side, rows] = part
                run_max[head, side, rows] = top

        def some_heads(step, carry):
            half = halves[0] if len(halves) == 1 else step % 2
            side = sides[0] if len(sides) == 1 else step // len(halves)
            work = []
            for i in range(HALF_HEADS):
                loaded = load(half, i)
                work += [(loaded, side, tile) for tile in range(ROWS // TILE)]
            scores = score(*work[0])
            for i, item in enumerate(work):
                following = score(*work[i + 1]) if i + 1 < len(work) else None
                absorb(*item, scores)
                scores = following
            if is_last:
                output(half, side).start()
            return carry

        lax.fori_loop(0, len(halves) * len(sides), some_heads, 0)

    def output(half, side):
        source = out_vm.at[side, :, pl.ds(pl.multiple_of(half * HALF_OUT, HALF_OUT), HALF_OUT)]
        target = out_hbm.at[0, :, lanes_of(core, half, CORE_OUT, HALF_OUT)]
        if side == 0:
            return pltpu.make_async_copy(source, target, out_sem.at[0, half])
        return remote(source, target, out_sem.at[1, half], out_sem.at[2, half], sibling)

    for copy in queries_in:
        copy.wait()
    attend([(0, 0)], sides=(0,), is_first=True)
    for swap in swaps[5:]:
        swap.wait_recv()
    attend([(0, 0)], sides=(1,), is_first=True)

    got(0, 1, POS)
    got(0, 1, H0)
    got(0, 2, H1)
    got(1, 0, POS)
    got(1, 0, H0)
    attend([(0, 1)], (H0,))
    attend([(0, 2)], (H1,))
    got(1, 0, H1)
    attend([(0, 1), (1, 0)], (H1,))
    attend([(0, 2), (1, 0)], (H0,))
    for kind in (POS, H0, H1):
        got(0, 3, kind)
    got(2, 0, POS)
    got(2, 0, H0)
    attend([(0, 3)])
    got(2, 0, H1)
    attend([(2, 0), (1, 1)], (H0,))
    attend([(2, 0), (1, 2)], (H1,))
    got(1, 1, H1)
    got(1, 2, H0)
    attend([(1, 1), (1, 3)], (H1,))
    got(2, 1, POS)
    got(2, 1, H0)
    got(2, 2, H1)
    attend([(1, 2), (1, 3)], (H0,))
    attend([(2, 1), (2, 2)])
    attend([(2, 3)], sides=(1,), is_last=True)
    attend([(2, 3)], sides=(0,), is_last=True)

    for half in range(2):
        output(half, 0).wait()
        output(half, 1).wait()
    for copy in swaps + started:
        copy.wait_send()


def copy_kernel(source, target, held, sems):
    parts = []
    for part in range(COPY_PARTS):
        rows = slice(part * 16, (part + 1) * 16)
        parts.append((
            pltpu.make_async_copy(source.at[0, rows], held.at[rows], sems.at[0, part]),
            pltpu.make_async_copy(held.at[rows], target.at[0, rows], sems.at[1, part])))
    for come, _ in parts:
        come.start()
    for come, leave in parts:
        come.wait()
        leave.start()
    for _, leave in parts:
        leave.wait()


def body(queries, keys, values, placement, lengths):
    any_spec = pl.BlockSpec(memory_space=pl.ANY)
    smem = pl.BlockSpec(memory_space=pltpu.SMEM)
    dma = pltpu.SemaphoreType.DMA
    out_shape = jax.ShapeDtypeStruct((1, TOK, KVH * GROUPS * HD), jnp.bfloat16)
    result = pl.pallas_call(
        kernel,
        out_shape=out_shape,
        in_specs=[any_spec, any_spec, any_spec, smem, smem],
        out_specs=any_spec,
        scratch_shapes=[
            pltpu.VMEM((3, NUM_X, 2, 2, CHIP_TOK, HALF_LANES), jnp.bfloat16),
            pltpu.VMEM((3, NUM_X, 32, TOK), jnp.int32),
            pltpu.VMEM((2, TOK, CORE_OUT), jnp.bfloat16),
            pltpu.VMEM((2, TOK, CORE_OUT), jnp.bfloat16),
            pltpu.VMEM((CORE_HEADS, 2, ROWS, 2 * HD), jnp.float32),
            pltpu.VMEM((CORE_HEADS, 2, ROWS, HD), jnp.float32),
            pltpu.VMEM((MAX_KEYS, HD), jnp.bfloat16),
            pltpu.VMEM((2, TILE, HD), jnp.bfloat16),
            dma((4, 2)),
            dma((7,)),
            dma((7,)),
            dma((3, 2)),
            dma((3, NUM_X, 3)),
            dma((2, NUM_X, 3)),
            dma((3, 2, 3, 3)),
        ],
        compiler_params=pltpu.CompilerParams(
            collective_id=0, has_side_effects=True, vmem_limit_bytes=56 * 1024 * 1024),
        cost_estimate=pl.CostEstimate(
            flops=4 * TOK * 64 * 3072 * HD, bytes_accessed=5 * 1024 * 1024,
            transcendentals=TOK * 64 * 3072),
    )(queries, keys, values, placement, lengths)
    return pl.pallas_call(
        copy_kernel,
        out_shape=out_shape,
        in_specs=[any_spec],
        out_specs=any_spec,
        scratch_shapes=[
            pltpu.VMEM((TOK, KVH * GROUPS * HD), jnp.bfloat16),
            dma((2, COPY_PARTS)),
        ],
        compiler_params=pltpu.CompilerParams(vmem_limit_bytes=56 * 1024 * 1024),
    )(result)


def solution(mesh):
    in_specs = (
        P("grp", "ctx", None),
        P("grp", "ctx", None),
        P("grp", "ctx", None),
        P("grp", "ctx"),
        P(),
    )
    out_specs = P("grp", "ctx", None)
    return jax.shard_map(body, mesh=mesh, in_specs=in_specs, out_specs=out_specs, check_vma=False)
```

```python
import math

import jax
import jax.numpy as jnp
from jax import lax
from jax.experimental import pallas as pl
from jax.experimental.pallas import tpu as pltpu
from jax.sharding import PartitionSpec as P

HD = 128
KVH = 8
GROUPS = 8
STRETCH = 64
TOK = 128
COL_STRETCHES = 16
REQS = 32
NUM_X = 4
NUM_GRP = 32
ROWS = GROUPS * TOK
TILE = 512
CORE_HEADS = KVH // 2
HALF_HEADS = CORE_HEADS // 2
HALF_LANES = HALF_HEADS * HD
CORE_LANES = CORE_HEADS * HD
HEAD_OUT = GROUPS * HD
HALF_OUT = HALF_HEADS * HEAD_OUT
CORE_OUT = CORE_HEADS * GROUPS * HD
CHIP_TOK = 2 * TOK
MAX_KEYS = 768
COPY_PARTS = TOK // 16

HIDDEN = -2e30
SCALE = math.log2(math.e) / math.sqrt(HD)
MESH = pl.DeviceIdType.MESH
H0, H1, POS, K1, V1 = 0, 1, 2, 3, 4


def kernel(q_hbm, k_hbm, v_hbm, place_ref, len_ref, out_hbm,
           kvbuf, pbuf, q_vm, out_vm, acc, run_max, extra, which,
           local_sem, swap_send, swap_recv, out_sem, recv_ici, send_z, send_x, send_own):
    ctx = lax.axis_index("ctx")
    grp = lax.axis_index("grp")
    x = ctx // 2
    core = ctx % 2
    right = (((x + 1) % NUM_X) * 2 + core, grp)
    left = (((x + NUM_X - 1) % NUM_X) * 2 + core, grp)
    sibling = (x * 2 + 1 - core, grp)
    after = (ctx, (grp + 1) % NUM_GRP)
    before = (ctx, (grp + NUM_GRP - 1) % NUM_GRP)

    def lanes_of(which_core, half, core_lanes, half_lanes):
        start = which_core * core_lanes + half * half_lanes
        return pl.ds(pl.multiple_of(start, half_lanes), half_lanes)

    local = []
    for half in range(2):
        for part, source in enumerate((k_hbm, v_hbm)):
            local.append(pltpu.make_async_copy(
                source.at[0, :, lanes_of(core, half, CORE_LANES, HALF_LANES)],
                kvbuf.at[0, 0, half, part, 0:TOK], local_sem.at[half, part]))
    queries_in = []
    for half in range(2):
        queries_in.append(pltpu.make_async_copy(
            q_hbm.at[0, :, lanes_of(core, half, CORE_OUT, HALF_OUT)],
            q_vm.at[0, :, half * HALF_OUT:(half + 1) * HALF_OUT], local_sem.at[2, half]))
    for copy in local + queries_in:
        copy.start()

    for slot in range(2):
        pbuf[0, 0, 8 * slot:8 * slot + 8] = jnp.full(
            (8, TOK), grp * COL_STRETCHES + place_ref[0, slot], jnp.int32)

    barrier = pltpu.get_barrier_semaphore()
    for device in (right, left, sibling, after, before):
        pl.semaphore_signal(barrier, inc=1, device_id=device, device_id_type=MESH)
    pl.semaphore_wait(barrier, 5)

    started = []

    def remote(src, dst, send_sem, recv_sem, device):
        return pltpu.make_async_remote_copy(
            src_ref=src, dst_ref=dst, send_sem=send_sem, recv_sem=recv_sem,
            device_id=device, device_id_type=MESH)

    swaps = [remote(pbuf.at[0, 0, 0:16], pbuf.at[0, 0, 16:32], swap_send.at[0], swap_recv.at[0], sibling)]
    for half in range(2):
        for part, source in enumerate((k_hbm, v_hbm)):
            i = 1 + 2 * half + part
            swaps.append(remote(
                source.at[0, :, lanes_of(1 - core, half, CORE_LANES, HALF_LANES)],
                kvbuf.at[0, 0, half, part, TOK:CHIP_TOK], swap_send.at[i], swap_recv.at[i], sibling))
    for half in range(2):
        swaps.append(remote(
            q_hbm.at[0, :, lanes_of(1 - core, half, CORE_OUT, HALF_OUT)],
            q_vm.at[1, :, half * HALF_OUT:(half + 1) * HALF_OUT],
            swap_send.at[5 + half], swap_recv.at[5 + half], sibling))
    for swap in swaps[:5]:
        swap.start()

    def unit(kind, d, rx):
        if kind == POS:
            return pbuf.at[d, rx]
        if kind in (K1, V1):
            return kvbuf.at[d, rx, H1, kind - K1]
        return kvbuf.at[d, rx, kind]

    def send(kind, src, dst, sem, device):
        copy = remote(unit(kind, *src), unit(kind, *dst), sem, recv_ici.at[dst[0], dst[1], kind], device)
        copy.start()
        started.append(copy)

    def to_after(d, rx, kind):
        send(kind, (d, rx), (d + 1, rx), send_z.at[d, rx, kind], after)

    def to_right(d, rx, kind):
        send(kind, (d, rx), (d, 1 if rx == 0 else 3), send_x.at[d, 0, rx, kind], right)

    def to_left(d, rx, kind):
        send(kind, (d, rx), (d, 2 if rx == 0 else 3), send_x.at[d, 1, rx, kind], left)

    def own_tokens(i, half, dst, device):
        for part, source in enumerate((k_hbm, v_hbm)):
            copy = remote(
                source.at[0, :, lanes_of(core, half, CORE_LANES, HALF_LANES)],
                kvbuf.at[dst[0], dst[1], half, part, 0:TOK],
                send_own.at[i, part], recv_ici.at[dst[0], dst[1], half], device)
            copy.start()
            started.append(copy)

    def swapped_tokens(i, half, dst, device):
        copy = remote(
            kvbuf.at[0, 0, half, :, TOK:CHIP_TOK], kvbuf.at[dst[0], dst[1], half, :, TOK:CHIP_TOK],
            send_own.at[i, 2], recv_ici.at[dst[0], dst[1], half], device)
        copy.start()
        started.append(copy)

    own_sends = (
        (H0, (0, 1), right), (H0, (1, 0), after), (H1, (0, 2), left),
        (H1, (1, 0), after), (H1, (0, 1), right), (H0, (0, 2), left))
    for i in range(3):
        own_tokens(i, *own_sends[i])
    swaps[0].wait_recv()
    to_right(0, 0, POS)
    to_left(0, 0, POS)
    to_after(0, 0, POS)
    for part in range(2):
        swaps[1 + part].wait_recv()
    swapped_tokens(0, *own_sends[0])
    swapped_tokens(1, *own_sends[1])
    for part in range(2):
        swaps[3 + part].wait_recv()
    swapped_tokens(2, *own_sends[2])
    for i in range(3, 6):
        own_tokens(i, *own_sends[i])
        swapped_tokens(i, *own_sends[i])
    for swap in swaps[5:]:
        swap.start()
    for copy in local:
        copy.wait()

    waited = set()
    for kind in (POS, H0, H1):
        waited.add((0, 0, kind))

    def got(d, rx, kind):
        if (d, rx, kind) in waited:
            return
        waited.add((d, rx, kind))
        ref = unit(kind, d, rx)
        remote(ref, ref, local_sem.at[3, 0], recv_ici.at[d, rx, kind], sibling).wait_recv()
        if d == 1 and rx == 0:
            if kind == POS:
                to_right(1, 0, POS)
                to_left(1, 0, POS)
                to_after(1, 0, POS)
            elif kind == H0:
                to_right(1, 0, H0)
                to_after(1, 0, H0)
            else:
                to_left(1, 0, H1)
                to_after(1, 0, H1)
                to_right(1, 0, H1)
                to_left(1, 0, H0)
        elif d == 2 and rx == 0:
            if kind == POS:
                to_right(2, 0, POS)
                to_left(2, 0, POS)
            elif kind == H1:
                got(2, 0, H0)
                to_right(2, 0, H1)
                to_left(2, 0, H1)
                to_right(2, 0, H0)
                to_left(2, 0, H0)
        elif d == 0 and rx == 1 and kind in (POS, H0):
            to_right(0, 1, kind)
        elif d == 0 and rx == 2 and kind == H1:
            to_left(0, 2, H1)
        elif d == 0 and rx == 3:
            to_after(0, 3, kind)
        elif d == 1 and rx == 3 and kind in (POS, H0):
            to_after(1, 3, kind)
        elif d == 2 and rx == 1 and kind == H1:
            to_right(2, 1, K1)
        elif d == 2 and rx == 2 and kind == H1:
            to_left(2, 2, V1)

    lane = lax.broadcasted_iota(jnp.int32, (8, TOK), 1)
    highs = jnp.full((8, TOK), -1, jnp.int32)
    for t in range(4):
        highs = jnp.where(lane == t, pbuf[0, 0, 8 * t:8 * t + 8, :], highs)
    lows = jnp.zeros((8, TOK), jnp.int32)
    end = jnp.int32(0)
    for r in range(REQS):
        end = end + len_ref[r]
        lows = jnp.where(end <= highs, end, lows)

    token = lax.broadcasted_iota(jnp.int32, (TILE, HD), 0) % TOK
    column = lax.broadcasted_iota(jnp.int32, (TILE, HD), 1)
    for side in range(2):
        which[side] = jnp.where(token // STRETCH + 2 * side == column, 1.0, 0.0).astype(jnp.bfloat16)

    def causal():
        row = lax.broadcasted_iota(jnp.int32, (TOK, TOK), 0)
        col = lax.broadcasted_iota(jnp.int32, (TOK, TOK), 1)
        later = (row // STRETCH == col // STRETCH) & (col > row)
        return jnp.where(later, HIDDEN, 0.0)

    def attend(chunks, halves=(H0, H1), sides=(0, 1), is_first=False, is_last=False):
        for d, rx in chunks:
            for kind in (POS,) + halves:
                if (d, rx, kind) == (2, 3, H1):
                    got(2, 3, K1)
                    got(2, 3, V1)
                else:
                    got(d, rx, kind)
        num_keys = CHIP_TOK * len(chunks)
        for i, (d, rx) in enumerate(chunks):
            for t in range(4):
                stretch = pbuf[d, rx, 8 * t:8 * t + 8, :]
                hide = jnp.where((stretch >= lows) & (stretch <= highs), 0.0, HIDDEN)
                at = i * CHIP_TOK + t * STRETCH
                extra[at:at + STRETCH, :] = jnp.concatenate([hide] * 8, axis=0).astype(jnp.bfloat16)

        def load(half, inner):
            lanes = slice(inner * HD, (inner + 1) * HD)
            keys = jnp.concatenate([kvbuf[d, rx, half, 0, :, lanes] for d, rx in chunks], axis=0)
            vals = jnp.concatenate([kvbuf[d, rx, half, 1, :, lanes] for d, rx in chunks], axis=0)
            keys = jnp.concatenate([keys, extra[:num_keys, :]], axis=1)
            vals = jnp.concatenate([vals, jnp.ones_like(vals)], axis=1)
            return half * HALF_HEADS + inner, keys, vals

        def score(loaded, side, tile):
            head, keys, _ = loaded
            queries = []
            for j in range(TILE // TOK):
                group = tile * (TILE // TOK) + j
                lanes = pl.ds(pl.multiple_of((head * GROUPS + group) * HD, HD), HD)
                queries.append(q_vm[side, :, lanes])
            queries = jnp.concatenate([jnp.concatenate(queries, axis=0), which[side]], axis=1)
            return lax.dot_general(
                queries, keys, (((1,), (1,)), ((), ())), preferred_element_type=jnp.float32)

        def absorb(loaded, side, tile, scores):
            head, _, vals = loaded
            rows = slice(tile * TILE, (tile + 1) * TILE)
            if is_first:
                own = scores[:, side * TOK:(side + 1) * TOK]
                own = (own.reshape(TILE // TOK, TOK, TOK) + causal()[None]).reshape(TILE, TOK)
                both = (own, scores[:, TOK:]) if side == 0 else (scores[:, :TOK], own)
                scores = jnp.concatenate(both, axis=1)
            top = jnp.broadcast_to(jnp.max(scores, axis=1, keepdims=True), (TILE, HD)) * SCALE
            if not is_first:
                old = run_max[head, side, rows]
                top = jnp.maximum(old, top)
            tops = jnp.concatenate([top] * (num_keys // HD), axis=1)
            weights = jnp.exp2(scores * SCALE - tops).astype(jnp.bfloat16)
            part = lax.dot_general(
                weights, vals, (((1,), (0,)), ((), ())),
                preferred_element_type=jnp.float32)
            if not is_first:
                factor = jnp.exp2(old - top)
                part = part + acc[head, side, rows] * jnp.concatenate([factor, factor], axis=1)
            if is_last:
                result = (part[:, :HD] / part[:, HD:]).astype(jnp.bfloat16)
                for j in range(TILE // TOK):
                    group = tile * (TILE // TOK) + j
                    place = pl.ds(pl.multiple_of((head * GROUPS + group) * HD, HD), HD)
                    out_vm[side, :, place] = result[j * TOK:(j + 1) * TOK]
            else:
                acc[head, side, rows] = part
                run_max[head, side, rows] = top

        def some_heads(step, carry):
            half = halves[0] if len(halves) == 1 else step % 2
            side = sides[0] if len(sides) == 1 else step // len(halves)
            work = []
            for i in range(HALF_HEADS):
                loaded = load(half, i)
                work += [(loaded, side, tile) for tile in range(ROWS // TILE)]
            scores = score(*work[0])
            for i, item in enumerate(work):
                following = score(*work[i + 1]) if i + 1 < len(work) else None
                absorb(*item, scores)
                scores = following
                if is_last and item[2] == ROWS // TILE - 1:
                    output(item[0][0], side).start()
            return carry

        lax.fori_loop(0, len(halves) * len(sides), some_heads, 0)

    def output(head, side):
        source = out_vm.at[side, :, pl.ds(head * HEAD_OUT, HEAD_OUT)]
        target = out_hbm.at[0, :, lanes_of(core, head, CORE_OUT, HEAD_OUT)]
        if side == 0:
            return pltpu.make_async_copy(source, target, out_sem.at[0, head])
        return remote(source, target, out_sem.at[1, head], out_sem.at[2, head], sibling)

    for copy in queries_in:
        copy.wait()
    attend([(0, 0)], sides=(0,), is_first=True)
    for swap in swaps[5:]:
        swap.wait_recv()
    attend([(0, 0)], sides=(1,), is_first=True)

    got(0, 1, POS)
    got(0, 1, H0)
    got(0, 2, H1)
    got(1, 0, POS)
    got(1, 0, H0)
    attend([(0, 1)], (H0,))
    attend([(0, 2)], (H1,))
    got(1, 0, H1)
    attend([(0, 1), (1, 0)], (H1,))
    attend([(0, 2), (1, 0)], (H0,))
    for kind in (POS, H0, H1):
        got(0, 3, kind)
    got(2, 0, POS)
    got(2, 0, H0)
    attend([(0, 3)])
    got(2, 0, H1)
    attend([(2, 0), (1, 1)], (H0,))
    attend([(2, 0), (1, 2)], (H1,))
    attend([(1, 2), (1, 3)], (H0,))
    got(2, 1, POS)
    got(2, 2, POS)
    got(2, 1, H1)
    got(2, 2, H1)
    attend([(1, 1), (1, 3)], (H1,))
    attend([(2, 1), (2, 2)], (H1,))
    for side in (1, 0):
        attend([(2, 1), (2, 2), (2, 3)], (H0,), sides=(side,), is_last=True)
    for side in (1, 0):
        attend([(2, 3)], (H1,), sides=(side,), is_last=True)

    for head in range(CORE_HEADS):
        output(head, 0).wait()
        output(head, 1).wait()
    for copy in swaps + started:
        copy.wait_send()


def copy_kernel(source, target, held, sems):
    parts = []
    for part in range(COPY_PARTS):
        rows = slice(part * 16, (part + 1) * 16)
        parts.append((
            pltpu.make_async_copy(source.at[0, rows], held.at[rows], sems.at[0, part]),
            pltpu.make_async_copy(held.at[rows], target.at[0, rows], sems.at[1, part])))
    for come, _ in parts:
        come.start()
    for come, leave in parts:
        come.wait()
        leave.start()
    for _, leave in parts:
        leave.wait()


def body(queries, keys, values, placement, lengths):
    any_spec = pl.BlockSpec(memory_space=pl.ANY)
    smem = pl.BlockSpec(memory_space=pltpu.SMEM)
    dma = pltpu.SemaphoreType.DMA
    out_shape = jax.ShapeDtypeStruct((1, TOK, KVH * GROUPS * HD), jnp.bfloat16)
    result = pl.pallas_call(
        kernel,
        out_shape=out_shape,
        in_specs=[any_spec, any_spec, any_spec, smem, smem],
        out_specs=any_spec,
        scratch_shapes=[
            pltpu.VMEM((3, NUM_X, 2, 2, CHIP_TOK, HALF_LANES), jnp.bfloat16),
            pltpu.VMEM((3, NUM_X, 32, TOK), jnp.int32),
            pltpu.VMEM((2, TOK, CORE_OUT), jnp.bfloat16),
            pltpu.VMEM((2, TOK, CORE_OUT), jnp.bfloat16),
            pltpu.VMEM((CORE_HEADS, 2, ROWS, 2 * HD), jnp.float32),
            pltpu.VMEM((CORE_HEADS, 2, ROWS, HD), jnp.float32),
            pltpu.VMEM((MAX_KEYS, HD), jnp.bfloat16),
            pltpu.VMEM((2, TILE, HD), jnp.bfloat16),
            dma((4, 2)),
            dma((7,)),
            dma((7,)),
            dma((3, CORE_HEADS)),
            dma((3, NUM_X, 5)),
            dma((2, NUM_X, 3)),
            dma((3, 2, 3, 5)),
            dma((6, 3)),
        ],
        compiler_params=pltpu.CompilerParams(
            collective_id=0, has_side_effects=True, vmem_limit_bytes=56 * 1024 * 1024),
        cost_estimate=pl.CostEstimate(
            flops=4 * TOK * 64 * 3072 * HD, bytes_accessed=5 * 1024 * 1024,
            transcendentals=TOK * 64 * 3072),
    )(queries, keys, values, placement, lengths)
    return pl.pallas_call(
        copy_kernel,
        out_shape=out_shape,
        in_specs=[any_spec],
        out_specs=any_spec,
        scratch_shapes=[
            pltpu.VMEM((TOK, KVH * GROUPS * HD), jnp.bfloat16),
            dma((2, COPY_PARTS)),
        ],
        compiler_params=pltpu.CompilerParams(vmem_limit_bytes=56 * 1024 * 1024),
    )(result)


def solution(mesh):
    in_specs = (
        P("grp", "ctx", None),
        P("grp", "ctx", None),
        P("grp", "ctx", None),
        P("grp", "ctx"),
        P(),
    )
    out_specs = P("grp", "ctx", None)
    return jax.shard_map(body, mesh=mesh, in_specs=in_specs, out_specs=out_specs, check_vma=False)
```

```python
import math

import jax
import jax.numpy as jnp
from jax import lax
from jax.experimental import pallas as pl
from jax.experimental.pallas import tpu as pltpu
from jax.sharding import PartitionSpec as P

HD = 128
KVH = 8
GROUPS = 8
STRETCH = 64
TOK = 128
COL_STRETCHES = 16
REQS = 32
NUM_X = 4
NUM_GRP = 32
ROWS = GROUPS * TOK
TILE = 512
CORE_HEADS = KVH // 2
HALF_HEADS = CORE_HEADS // 2
HALF_LANES = HALF_HEADS * HD
CORE_LANES = CORE_HEADS * HD
HEAD_OUT = GROUPS * HD
HALF_OUT = HALF_HEADS * HEAD_OUT
CORE_OUT = CORE_HEADS * GROUPS * HD
CHIP_TOK = 2 * TOK
MAX_KEYS = 768
COPY_PARTS = TOK // 16

HIDDEN = -2e30
SCALE = math.log2(math.e) / math.sqrt(HD)
MESH = pl.DeviceIdType.MESH
H0, H1, POS = 0, 1, 2


def kernel(q_hbm, k_hbm, v_hbm, place_ref, len_ref, out_hbm,
           kvbuf, pbuf, q_vm, out_vm, acc, run_max, extra, which,
           local_sem, swap_send, swap_recv, out_sem, recv_ici, send_z, send_x, send_own):
    ctx = lax.axis_index("ctx")
    grp = lax.axis_index("grp")
    x = ctx // 2
    core = ctx % 2
    right = (((x + 1) % NUM_X) * 2 + core, grp)
    left = (((x + NUM_X - 1) % NUM_X) * 2 + core, grp)
    sibling = (x * 2 + 1 - core, grp)
    after = (ctx, (grp + 1) % NUM_GRP)
    before = (ctx, (grp + NUM_GRP - 1) % NUM_GRP)

    barrier = pltpu.get_barrier_semaphore()
    for device in (right, left, sibling, after, before):
        pl.semaphore_signal(barrier, inc=1, device_id=device, device_id_type=MESH)

    def lanes_of(which_core, half, core_lanes, half_lanes):
        start = which_core * core_lanes + half * half_lanes
        return pl.ds(pl.multiple_of(start, half_lanes), half_lanes)

    local = []
    for half in range(2):
        for part, source in enumerate((k_hbm, v_hbm)):
            local.append(pltpu.make_async_copy(
                source.at[0, :, lanes_of(core, half, CORE_LANES, HALF_LANES)],
                kvbuf.at[0, 0, half, part, 0:TOK], local_sem.at[half, part]))
    queries_in = []
    for half in range(2):
        queries_in.append(pltpu.make_async_copy(
            q_hbm.at[0, :, lanes_of(core, half, CORE_OUT, HALF_OUT)],
            q_vm.at[0, :, half * HALF_OUT:(half + 1) * HALF_OUT], local_sem.at[2, half]))
    for copy in local + queries_in:
        copy.start()

    for slot in range(2):
        pbuf[0, 0, 8 * slot:8 * slot + 8] = jnp.full(
            (8, TOK), grp * COL_STRETCHES + place_ref[0, slot], jnp.int32)

    pl.semaphore_wait(barrier, 5)

    started = []

    def remote(src, dst, send_sem, recv_sem, device):
        return pltpu.make_async_remote_copy(
            src_ref=src, dst_ref=dst, send_sem=send_sem, recv_sem=recv_sem,
            device_id=device, device_id_type=MESH)

    swaps = [remote(pbuf.at[0, 0, 0:16], pbuf.at[0, 0, 16:32], swap_send.at[0], swap_recv.at[0], sibling)]
    for half in range(2):
        for part, source in enumerate((k_hbm, v_hbm)):
            i = 1 + 2 * half + part
            swaps.append(remote(
                source.at[0, :, lanes_of(1 - core, half, CORE_LANES, HALF_LANES)],
                kvbuf.at[0, 0, half, part, TOK:CHIP_TOK], swap_send.at[i], swap_recv.at[i], sibling))
    for half in range(2):
        swaps.append(remote(
            q_hbm.at[0, :, lanes_of(1 - core, half, CORE_OUT, HALF_OUT)],
            q_vm.at[1, :, half * HALF_OUT:(half + 1) * HALF_OUT],
            swap_send.at[5 + half], swap_recv.at[5 + half], sibling))
    for swap in swaps[:5]:
        swap.start()

    def unit(kind, d, rx):
        if kind == POS:
            return pbuf.at[d, rx]
        return kvbuf.at[d, rx, kind]

    def send(kind, src, dst, sem, device):
        copy = remote(unit(kind, *src), unit(kind, *dst), sem, recv_ici.at[dst[0], dst[1], kind], device)
        copy.start()
        started.append(copy)

    def to_after(d, rx, kind):
        send(kind, (d, rx), (d + 1, rx), send_z.at[d, rx, kind], after)

    def to_right(d, rx, kind):
        send(kind, (d, rx), (d, 1 if rx == 0 else 3), send_x.at[d, 0, rx, kind], right)

    def to_left(d, rx, kind):
        send(kind, (d, rx), (d, 2 if rx == 0 else 3), send_x.at[d, 1, rx, kind], left)

    def own_tokens(i, half, dst, device):
        for part, source in enumerate((k_hbm, v_hbm)):
            copy = remote(
                source.at[0, :, lanes_of(core, half, CORE_LANES, HALF_LANES)],
                kvbuf.at[dst[0], dst[1], half, part, 0:TOK],
                send_own.at[i, part], recv_ici.at[dst[0], dst[1], half], device)
            copy.start()
            started.append(copy)

    def swapped_tokens(i, half, dst, device):
        copy = remote(
            kvbuf.at[0, 0, half, :, TOK:CHIP_TOK], kvbuf.at[dst[0], dst[1], half, :, TOK:CHIP_TOK],
            send_own.at[i, 2], recv_ici.at[dst[0], dst[1], half], device)
        copy.start()
        started.append(copy)

    own_sends = (
        (H0, (0, 1), right), (H0, (1, 0), after), (H1, (0, 2), left),
        (H1, (1, 0), after), (H1, (0, 1), right), (H0, (0, 2), left))
    for i in range(3):
        own_tokens(i, *own_sends[i])
    swaps[0].wait_recv()
    to_right(0, 0, POS)
    to_left(0, 0, POS)
    to_after(0, 0, POS)
    for part in range(2):
        swaps[1 + part].wait_recv()
    swapped_tokens(0, *own_sends[0])
    swapped_tokens(1, *own_sends[1])
    for part in range(2):
        swaps[3 + part].wait_recv()
    swapped_tokens(2, *own_sends[2])
    for swap in swaps[5:]:
        swap.start()
    for i in range(3, 6):
        own_tokens(i, *own_sends[i])
        swapped_tokens(i, *own_sends[i])
    for copy in local:
        copy.wait()

    waited = set()
    for kind in (POS, H0, H1):
        waited.add((0, 0, kind))

    def got(d, rx, kind):
        if (d, rx, kind) in waited:
            return
        waited.add((d, rx, kind))
        ref = unit(kind, d, rx)
        remote(ref, ref, local_sem.at[3, 0], recv_ici.at[d, rx, kind], sibling).wait_recv()
        if d == 1 and rx == 0:
            if kind == POS:
                to_right(1, 0, POS)
                to_left(1, 0, POS)
                to_after(1, 0, POS)
            elif kind == H0:
                to_right(1, 0, H0)
                to_after(1, 0, H0)
            else:
                to_left(1, 0, H1)
                to_after(1, 0, H1)
                to_right(1, 0, H1)
                to_left(1, 0, H0)
        elif d == 2 and rx == 0:
            if kind == POS:
                to_right(2, 0, POS)
                to_left(2, 0, POS)
            elif kind == H1:
                got(2, 0, H0)
                to_right(2, 0, H1)
                to_left(2, 0, H1)
                to_right(2, 0, H0)
                to_left(2, 0, H0)
        elif d == 0 and rx == 1 and kind in (POS, H0):
            to_right(0, 1, kind)
        elif d == 0 and rx == 2 and kind == H1:
            to_left(0, 2, H1)
        elif d == 0 and rx == 3:
            to_after(0, 3, kind)
        elif d == 1 and rx == 3:
            to_after(1, 3, kind)

    lane = lax.broadcasted_iota(jnp.int32, (8, TOK), 1)
    highs = jnp.full((8, TOK), -1, jnp.int32)
    for t in range(4):
        highs = jnp.where(lane == t, pbuf[0, 0, 8 * t:8 * t + 8, :], highs)
    lows = jnp.zeros((8, TOK), jnp.int32)
    end = jnp.int32(0)
    for r in range(REQS):
        end = end + len_ref[r]
        lows = jnp.where(end <= highs, end, lows)

    token = lax.broadcasted_iota(jnp.int32, (TILE, HD), 0) % TOK
    column = lax.broadcasted_iota(jnp.int32, (TILE, HD), 1)
    for side in range(2):
        which[side] = jnp.where(token // STRETCH + 2 * side == column, 1.0, 0.0).astype(jnp.bfloat16)

    def causal():
        row = lax.broadcasted_iota(jnp.int32, (TOK, TOK), 0)
        col = lax.broadcasted_iota(jnp.int32, (TOK, TOK), 1)
        later = (row // STRETCH == col // STRETCH) & (col > row)
        return jnp.where(later, HIDDEN, 0.0)

    def attend(chunks, halves=(H0, H1), sides=(0, 1), is_first=False, is_last=False):
        for d, rx in chunks:
            for kind in (POS,) + halves:
                got(d, rx, kind)
        num_keys = CHIP_TOK * len(chunks)
        for i, (d, rx) in enumerate(chunks):
            for t in range(4):
                stretch = pbuf[d, rx, 8 * t:8 * t + 8, :]
                hide = jnp.where((stretch >= lows) & (stretch <= highs), 0.0, HIDDEN)
                at = i * CHIP_TOK + t * STRETCH
                extra[at:at + STRETCH, :] = jnp.concatenate([hide] * 8, axis=0).astype(jnp.bfloat16)

        def load(half, inner):
            lanes = slice(inner * HD, (inner + 1) * HD)
            keys = jnp.concatenate([kvbuf[d, rx, half, 0, :, lanes] for d, rx in chunks], axis=0)
            vals = jnp.concatenate([kvbuf[d, rx, half, 1, :, lanes] for d, rx in chunks], axis=0)
            keys = jnp.concatenate([keys, extra[:num_keys, :]], axis=1)
            vals = jnp.concatenate([vals, jnp.ones_like(vals)], axis=1)
            return half * HALF_HEADS + inner, keys, vals

        def score(loaded, side, tile):
            head, keys, _ = loaded
            queries = []
            for j in range(TILE // TOK):
                group = tile * (TILE // TOK) + j
                lanes = pl.ds(pl.multiple_of((head * GROUPS + group) * HD, HD), HD)
                queries.append(q_vm[side, :, lanes])
            queries = jnp.concatenate([jnp.concatenate(queries, axis=0), which[side]], axis=1)
            return lax.dot_general(
                queries, keys, (((1,), (1,)), ((), ())), preferred_element_type=jnp.float32)

        def absorb(loaded, side, tile, scores):
            head, _, vals = loaded
            rows = slice(tile * TILE, (tile + 1) * TILE)
            if is_first:
                own = scores[:, side * TOK:(side + 1) * TOK]
                own = (own.reshape(TILE // TOK, TOK, TOK) + causal()[None]).reshape(TILE, TOK)
                both = (own, scores[:, TOK:]) if side == 0 else (scores[:, :TOK], own)
                scores = jnp.concatenate(both, axis=1)
            top = jnp.broadcast_to(jnp.max(scores, axis=1, keepdims=True), (TILE, HD)) * SCALE
            if not is_first:
                old = run_max[head, side, rows]
                top = jnp.maximum(old, top)
            tops = jnp.concatenate([top] * (num_keys // HD), axis=1)
            weights = jnp.exp2(scores * SCALE - tops).astype(jnp.bfloat16)
            part = lax.dot_general(
                weights, vals, (((1,), (0,)), ((), ())),
                preferred_element_type=jnp.float32)
            if not is_first:
                factor = jnp.exp2(old - top)
                part = part + acc[head, side, rows] * jnp.concatenate([factor, factor], axis=1)
            if is_last:
                result = (part[:, :HD] / part[:, HD:]).astype(jnp.bfloat16)
                for j in range(TILE // TOK):
                    group = tile * (TILE // TOK) + j
                    place = pl.ds(pl.multiple_of((head * GROUPS + group) * HD, HD), HD)
                    out_vm[side, :, place] = result[j * TOK:(j + 1) * TOK]
            else:
                acc[head, side, rows] = part
                run_max[head, side, rows] = top

        def some_heads(step, carry):
            half = halves[0] if len(halves) == 1 else step % 2
            side = sides[0] if len(sides) == 1 else step // len(halves)
            work = []
            for i in range(HALF_HEADS):
                loaded = load(half, i)
                work += [(loaded, side, tile) for tile in range(ROWS // TILE)]
            scores = score(*work[0])
            for i, item in enumerate(work):
                following = score(*work[i + 1]) if i + 1 < len(work) else None
                absorb(*item, scores)
                scores = following
                if is_last and item[2] == ROWS // TILE - 1:
                    output(item[0][0], side).start()
            return carry

        lax.fori_loop(0, len(halves) * len(sides), some_heads, 0)

    def output(head, side):
        source = out_vm.at[side, :, pl.ds(head * HEAD_OUT, HEAD_OUT)]
        target = out_hbm.at[0, :, lanes_of(core, head, CORE_OUT, HEAD_OUT)]
        if side == 0:
            return pltpu.make_async_copy(source, target, out_sem.at[0, head])
        return remote(source, target, out_sem.at[1, head], out_sem.at[2, head], sibling)

    for copy in queries_in:
        copy.wait()
    attend([(0, 0)], sides=(0,), is_first=True)
    got(0, 1, POS)
    got(0, 1, H0)
    got(0, 2, H1)
    got(1, 0, POS)
    got(1, 0, H0)
    for swap in swaps[5:]:
        swap.wait_recv()
    attend([(0, 0)], sides=(1,), is_first=True)
    attend([(0, 1)], (H0,))
    attend([(0, 2)], (H1,))
    got(1, 0, H1)
    attend([(0, 1), (1, 0)], (H1,))
    attend([(0, 2), (1, 0)], (H0,))
    for kind in (POS, H0, H1):
        got(0, 3, kind)
    got(2, 0, POS)
    got(2, 0, H0)
    attend([(0, 3)])
    got(2, 0, H1)
    attend([(2, 0), (1, 1)], (H0,))
    attend([(2, 0), (1, 2)], (H1,))
    attend([(1, 2), (1, 3)], (H0,))
    got(2, 1, POS)
    got(2, 2, POS)
    got(2, 1, H1)
    got(2, 2, H1)
    attend([(1, 1), (1, 3)], (H1,))
    attend([(2, 1), (2, 2)], (H1,))
    for side in (1, 0):
        attend([(2, 1), (2, 2), (2, 3)], (H0,), sides=(side,), is_last=True)
    for side in (1, 0):
        attend([(2, 3)], (H1,), sides=(side,), is_last=True)

    for head in range(CORE_HEADS):
        output(head, 0).wait()
        output(head, 1).wait()
    for copy in swaps + started:
        copy.wait_send()


def copy_kernel(source, target, held, sems):
    parts = []
    for part in range(COPY_PARTS):
        rows = slice(part * 16, (part + 1) * 16)
        parts.append((
            pltpu.make_async_copy(source.at[0, rows], held.at[rows], sems.at[0, part]),
            pltpu.make_async_copy(held.at[rows], target.at[0, rows], sems.at[1, part])))
    for come, _ in parts:
        come.start()
    for come, leave in parts:
        come.wait()
        leave.start()
    for _, leave in parts:
        leave.wait()


def body(queries, keys, values, placement, lengths):
    any_spec = pl.BlockSpec(memory_space=pl.ANY)
    smem = pl.BlockSpec(memory_space=pltpu.SMEM)
    dma = pltpu.SemaphoreType.DMA
    out_shape = jax.ShapeDtypeStruct((1, TOK, KVH * GROUPS * HD), jnp.bfloat16)
    result = pl.pallas_call(
        kernel,
        out_shape=out_shape,
        in_specs=[any_spec, any_spec, any_spec, smem, smem],
        out_specs=any_spec,
        scratch_shapes=[
            pltpu.VMEM((3, NUM_X, 2, 2, CHIP_TOK, HALF_LANES), jnp.bfloat16),
            pltpu.VMEM((3, NUM_X, 32, TOK), jnp.int32),
            pltpu.VMEM((2, TOK, CORE_OUT), jnp.bfloat16),
            pltpu.VMEM((2, TOK, CORE_OUT), jnp.bfloat16),
            pltpu.VMEM((CORE_HEADS, 2, ROWS, 2 * HD), jnp.float32),
            pltpu.VMEM((CORE_HEADS, 2, ROWS, HD), jnp.float32),
            pltpu.VMEM((MAX_KEYS, HD), jnp.bfloat16),
            pltpu.VMEM((2, TILE, HD), jnp.bfloat16),
            dma((4, 2)),
            dma((7,)),
            dma((7,)),
            dma((3, CORE_HEADS)),
            dma((3, NUM_X, 3)),
            dma((2, NUM_X, 3)),
            dma((3, 2, 3, 3)),
            dma((6, 3)),
        ],
        compiler_params=pltpu.CompilerParams(
            collective_id=0, has_side_effects=True, vmem_limit_bytes=56 * 1024 * 1024),
        cost_estimate=pl.CostEstimate(
            flops=4 * TOK * 64 * 3072 * HD, bytes_accessed=5 * 1024 * 1024,
            transcendentals=TOK * 64 * 3072),
    )(queries, keys, values, placement, lengths)
    return pl.pallas_call(
        copy_kernel,
        out_shape=out_shape,
        in_specs=[any_spec],
        out_specs=any_spec,
        scratch_shapes=[
            pltpu.VMEM((TOK, KVH * GROUPS * HD), jnp.bfloat16),
            dma((2, COPY_PARTS)),
        ],
        compiler_params=pltpu.CompilerParams(vmem_limit_bytes=56 * 1024 * 1024),
    )(result)


def solution(mesh):
    in_specs = (
        P("grp", "ctx", None),
        P("grp", "ctx", None),
        P("grp", "ctx", None),
        P("grp", "ctx"),
        P(),
    )
    out_specs = P("grp", "ctx", None)
    return jax.shard_map(body, mesh=mesh, in_specs=in_specs, out_specs=out_specs, check_vma=False)
```

```python
import math

import jax
import jax.numpy as jnp
from jax import lax
from jax.experimental import pallas as pl
from jax.experimental.pallas import tpu as pltpu
from jax.sharding import PartitionSpec as P

HD = 128
KVH = 8
GROUPS = 8
STRETCH = 64
TOK = 128
COL_STRETCHES = 16
REQS = 32
NUM_X = 4
NUM_GRP = 32
ROWS = GROUPS * TOK
TILE = 512
CORE_HEADS = KVH // 2
HALF_HEADS = CORE_HEADS // 2
HALF_LANES = HALF_HEADS * HD
CORE_LANES = CORE_HEADS * HD
HEAD_OUT = GROUPS * HD
HALF_OUT = HALF_HEADS * HEAD_OUT
CORE_OUT = CORE_HEADS * GROUPS * HD
CHIP_TOK = 2 * TOK
MAX_KEYS = 768
COPY_PARTS = TOK // 16

HIDDEN = -2e30
SCALE = math.log2(math.e) / math.sqrt(HD)
MESH = pl.DeviceIdType.MESH
H0, H1, POS, K1, V1 = 0, 1, 2, 3, 4


def kernel(q_hbm, k_hbm, v_hbm, place_ref, len_ref, out_hbm,
           kvbuf, pbuf, q_vm, out_vm, acc, run_max, extra, which,
           local_sem, swap_send, swap_recv, out_sem, recv_ici, send_z, send_x, send_own):
    ctx = lax.axis_index("ctx")
    grp = lax.axis_index("grp")
    x = ctx // 2
    core = ctx % 2
    right = (((x + 1) % NUM_X) * 2 + core, grp)
    left = (((x + NUM_X - 1) % NUM_X) * 2 + core, grp)
    sibling = (x * 2 + 1 - core, grp)
    after = (ctx, (grp + 1) % NUM_GRP)
    before = (ctx, (grp + NUM_GRP - 1) % NUM_GRP)

    barrier = pltpu.get_barrier_semaphore()
    for device in (right, left, sibling, after, before):
        pl.semaphore_signal(barrier, inc=1, device_id=device, device_id_type=MESH)

    def lanes_of(which_core, half, core_lanes, half_lanes):
        start = which_core * core_lanes + half * half_lanes
        return pl.ds(pl.multiple_of(start, half_lanes), half_lanes)

    local = []
    for half in range(2):
        for part, source in enumerate((k_hbm, v_hbm)):
            local.append(pltpu.make_async_copy(
                source.at[0, :, lanes_of(core, half, CORE_LANES, HALF_LANES)],
                kvbuf.at[0, 0, half, part, 0:TOK], local_sem.at[half, part]))
    queries_in = []
    for half in range(2):
        queries_in.append(pltpu.make_async_copy(
            q_hbm.at[0, :, lanes_of(core, half, CORE_OUT, HALF_OUT)],
            q_vm.at[0, :, half * HALF_OUT:(half + 1) * HALF_OUT], local_sem.at[2, half]))
    for copy in local + queries_in:
        copy.start()

    for slot in range(2):
        pbuf[0, 0, 8 * slot:8 * slot + 8] = jnp.full(
            (8, TOK), grp * COL_STRETCHES + place_ref[0, slot], jnp.int32)

    pl.semaphore_wait(barrier, 5)

    started = []

    def remote(src, dst, send_sem, recv_sem, device):
        return pltpu.make_async_remote_copy(
            src_ref=src, dst_ref=dst, send_sem=send_sem, recv_sem=recv_sem,
            device_id=device, device_id_type=MESH)

    swaps = [remote(pbuf.at[0, 0, 0:16], pbuf.at[0, 0, 16:32], swap_send.at[0], swap_recv.at[0], sibling)]
    for half in range(2):
        for part, source in enumerate((k_hbm, v_hbm)):
            i = 1 + 2 * half + part
            swaps.append(remote(
                source.at[0, :, lanes_of(1 - core, half, CORE_LANES, HALF_LANES)],
                kvbuf.at[0, 0, half, part, TOK:CHIP_TOK], swap_send.at[i], swap_recv.at[i], sibling))
    for half in range(2):
        swaps.append(remote(
            q_hbm.at[0, :, lanes_of(1 - core, half, CORE_OUT, HALF_OUT)],
            q_vm.at[1, :, half * HALF_OUT:(half + 1) * HALF_OUT],
            swap_send.at[5 + half], swap_recv.at[5 + half], sibling))
    for swap in swaps[:5]:
        swap.start()

    def unit(kind, d, rx):
        if kind == POS:
            return pbuf.at[d, rx]
        if kind in (K1, V1):
            return kvbuf.at[d, rx, H1, kind - K1]
        return kvbuf.at[d, rx, kind]

    def send(kind, src, dst, sem, device):
        copy = remote(unit(kind, *src), unit(kind, *dst), sem, recv_ici.at[dst[0], dst[1], kind], device)
        copy.start()
        started.append(copy)

    def to_after(d, rx, kind):
        send(kind, (d, rx), (d + 1, rx), send_z.at[d, rx, kind], after)

    def to_right(d, rx, kind):
        send(kind, (d, rx), (d, 1 if rx == 0 else 3), send_x.at[d, 0, rx, kind], right)

    def to_left(d, rx, kind):
        send(kind, (d, rx), (d, 2 if rx == 0 else 3), send_x.at[d, 1, rx, kind], left)

    def own_tokens(i, half, dst, device):
        for part, source in enumerate((k_hbm, v_hbm)):
            copy = remote(
                source.at[0, :, lanes_of(core, half, CORE_LANES, HALF_LANES)],
                kvbuf.at[dst[0], dst[1], half, part, 0:TOK],
                send_own.at[i, part], recv_ici.at[dst[0], dst[1], half], device)
            copy.start()
            started.append(copy)

    def swapped_tokens(i, half, dst, device):
        copy = remote(
            kvbuf.at[0, 0, half, :, TOK:CHIP_TOK], kvbuf.at[dst[0], dst[1], half, :, TOK:CHIP_TOK],
            send_own.at[i, 2], recv_ici.at[dst[0], dst[1], half], device)
        copy.start()
        started.append(copy)

    own_sends = (
        (H0, (0, 1), right), (H0, (1, 0), after), (H1, (0, 2), left),
        (H1, (1, 0), after), (H1, (0, 1), right), (H0, (0, 2), left))
    for i in range(3):
        own_tokens(i, *own_sends[i])
    swaps[0].wait_recv()
    to_right(0, 0, POS)
    to_left(0, 0, POS)
    to_after(0, 0, POS)
    for part in range(2):
        swaps[1 + part].wait_recv()
    swapped_tokens(0, *own_sends[0])
    swapped_tokens(1, *own_sends[1])
    for part in range(2):
        swaps[3 + part].wait_recv()
    swapped_tokens(2, *own_sends[2])
    for swap in swaps[5:]:
        swap.start()
    for i in range(3, 6):
        own_tokens(i, *own_sends[i])
        swapped_tokens(i, *own_sends[i])
    for copy in local:
        copy.wait()

    waited = set()
    for kind in (POS, H0, H1):
        waited.add((0, 0, kind))

    def got(d, rx, kind):
        if (d, rx, kind) in waited:
            return
        waited.add((d, rx, kind))
        ref = unit(kind, d, rx)
        remote(ref, ref, local_sem.at[3, 0], recv_ici.at[d, rx, kind], sibling).wait_recv()
        if d == 1 and rx == 0:
            if kind == POS:
                to_right(1, 0, POS)
                to_left(1, 0, POS)
                to_after(1, 0, POS)
            elif kind == H0:
                to_right(1, 0, H0)
                to_after(1, 0, H0)
            else:
                to_left(1, 0, H1)
                to_after(1, 0, H1)
                to_right(1, 0, H1)
                to_left(1, 0, H0)
        elif d == 2 and rx == 0:
            if kind == POS:
                to_right(2, 0, POS)
                to_left(2, 0, POS)
            elif kind == H1:
                got(2, 0, H0)
                to_right(2, 0, H1)
                to_left(2, 0, H1)
                to_right(2, 0, H0)
                to_left(2, 0, H0)
        elif d == 0 and rx == 1 and kind in (POS, H0):
            to_right(0, 1, kind)
        elif d == 0 and rx == 2 and kind == H1:
            to_left(0, 2, H1)
        elif d == 0 and rx == 3:
            to_after(0, 3, kind)
        elif d == 1 and rx == 3 and kind in (POS, H0):
            to_after(1, 3, kind)
        elif d == 2 and rx == 1 and kind == H1:
            to_right(2, 1, K1)
        elif d == 2 and rx == 2 and kind == H1:
            to_left(2, 2, V1)

    lane = lax.broadcasted_iota(jnp.int32, (8, TOK), 1)
    highs = jnp.full((8, TOK), -1, jnp.int32)
    for t in range(4):
        highs = jnp.where(lane == t, pbuf[0, 0, 8 * t:8 * t + 8, :], highs)
    lows = jnp.zeros((8, TOK), jnp.int32)
    end = jnp.int32(0)
    for r in range(REQS):
        end = end + len_ref[r]
        lows = jnp.where(end <= highs, end, lows)

    token = lax.broadcasted_iota(jnp.int32, (TILE, HD), 0) % TOK
    column = lax.broadcasted_iota(jnp.int32, (TILE, HD), 1)
    for side in range(2):
        which[side] = jnp.where(token // STRETCH + 2 * side == column, 1.0, 0.0).astype(jnp.bfloat16)

    def causal():
        row = lax.broadcasted_iota(jnp.int32, (TOK, TOK), 0)
        col = lax.broadcasted_iota(jnp.int32, (TOK, TOK), 1)
        later = (row // STRETCH == col // STRETCH) & (col > row)
        return jnp.where(later, HIDDEN, 0.0)

    def attend(chunks, halves=(H0, H1), sides=(0, 1), is_first=False, is_last=False):
        for d, rx in chunks:
            for kind in (POS,) + halves:
                if (d, rx, kind) == (2, 3, H1):
                    got(2, 3, K1)
                    got(2, 3, V1)
                else:
                    got(d, rx, kind)
        num_keys = CHIP_TOK * len(chunks)
        for i, (d, rx) in enumerate(chunks):
            for t in range(4):
                stretch = pbuf[d, rx, 8 * t:8 * t + 8, :]
                hide = jnp.where((stretch >= lows) & (stretch <= highs), 0.0, HIDDEN)
                at = i * CHIP_TOK + t * STRETCH
                extra[at:at + STRETCH, :] = jnp.concatenate([hide] * 8, axis=0).astype(jnp.bfloat16)

        def load(half, inner):
            lanes = slice(inner * HD, (inner + 1) * HD)
            keys = jnp.concatenate([kvbuf[d, rx, half, 0, :, lanes] for d, rx in chunks], axis=0)
            vals = jnp.concatenate([kvbuf[d, rx, half, 1, :, lanes] for d, rx in chunks], axis=0)
            keys = jnp.concatenate([keys, extra[:num_keys, :]], axis=1)
            vals = jnp.concatenate([vals, jnp.ones_like(vals)], axis=1)
            return half * HALF_HEADS + inner, keys, vals

        def score(loaded, side, tile):
            head, keys, _ = loaded
            queries = []
            for j in range(TILE // TOK):
                group = tile * (TILE // TOK) + j
                lanes = pl.ds(pl.multiple_of((head * GROUPS + group) * HD, HD), HD)
                queries.append(q_vm[side, :, lanes])
            queries = jnp.concatenate([jnp.concatenate(queries, axis=0), which[side]], axis=1)
            return lax.dot_general(
                queries, keys, (((1,), (1,)), ((), ())), preferred_element_type=jnp.float32)

        def absorb(loaded, side, tile, scores):
            head, _, vals = loaded
            rows = slice(tile * TILE, (tile + 1) * TILE)
            if is_first:
                own = scores[:, side * TOK:(side + 1) * TOK]
                own = (own.reshape(TILE // TOK, TOK, TOK) + causal()[None]).reshape(TILE, TOK)
                both = (own, scores[:, TOK:]) if side == 0 else (scores[:, :TOK], own)
                scores = jnp.concatenate(both, axis=1)
            top = jnp.broadcast_to(jnp.max(scores, axis=1, keepdims=True), (TILE, HD)) * SCALE
            if not is_first:
                old = run_max[head, side, rows]
                top = jnp.maximum(old, top)
            tops = jnp.concatenate([top] * (num_keys // HD), axis=1)
            weights = jnp.exp2(scores * SCALE - tops).astype(jnp.bfloat16)
            part = lax.dot_general(
                weights, vals, (((1,), (0,)), ((), ())),
                preferred_element_type=jnp.float32)
            if not is_first:
                factor = jnp.exp2(old - top)
                part = part + acc[head, side, rows] * jnp.concatenate([factor, factor], axis=1)
            if is_last:
                result = (part[:, :HD] / part[:, HD:]).astype(jnp.bfloat16)
                for j in range(TILE // TOK):
                    group = tile * (TILE // TOK) + j
                    place = pl.ds(pl.multiple_of((head * GROUPS + group) * HD, HD), HD)
                    out_vm[side, :, place] = result[j * TOK:(j + 1) * TOK]
            else:
                acc[head, side, rows] = part
                run_max[head, side, rows] = top

        def some_heads(step, carry):
            half = halves[0] if len(halves) == 1 else step % 2
            side = sides[0] if len(sides) == 1 else step // len(halves)
            work = []
            for i in range(HALF_HEADS):
                loaded = load(half, i)
                work += [(loaded, side, tile) for tile in range(ROWS // TILE)]
            scores = score(*work[0])
            for i, item in enumerate(work):
                following = score(*work[i + 1]) if i + 1 < len(work) else None
                absorb(*item, scores)
                scores = following
                if is_last and item[2] == ROWS // TILE - 1:
                    output(item[0][0], side).start()
            return carry

        lax.fori_loop(0, len(halves) * len(sides), some_heads, 0)

    def output(head, side):
        source = out_vm.at[side, :, pl.ds(head * HEAD_OUT, HEAD_OUT)]
        target = out_hbm.at[0, :, lanes_of(core, head, CORE_OUT, HEAD_OUT)]
        if side == 0:
            return pltpu.make_async_copy(source, target, out_sem.at[0, head])
        return remote(source, target, out_sem.at[1, head], out_sem.at[2, head], sibling)

    for copy in queries_in:
        copy.wait()
    attend([(0, 0)], sides=(0,), is_first=True)
    got(0, 1, POS)
    got(0, 1, H0)
    got(0, 2, H1)
    got(1, 0, POS)
    got(1, 0, H0)
    for swap in swaps[5:]:
        swap.wait_recv()
    attend([(0, 0)], sides=(1,), is_first=True)
    attend([(0, 1)], (H0,))
    attend([(0, 2)], (H1,))
    got(1, 0, H1)
    attend([(0, 1), (1, 0)], (H1,))
    attend([(0, 2), (1, 0)], (H0,))
    for kind in (POS, H0, H1):
        got(0, 3, kind)
    got(2, 0, POS)
    got(2, 0, H0)
    attend([(0, 3)])
    got(2, 0, H1)
    attend([(2, 0), (1, 1)], (H0,))
    attend([(2, 0), (1, 2)], (H1,))
    attend([(1, 2), (1, 3)], (H0,))
    got(2, 1, POS)
    got(2, 2, POS)
    got(2, 1, H1)
    got(2, 2, H1)
    attend([(1, 1), (1, 3)], (H1,))
    attend([(2, 1), (2, 2)], (H1,))
    for side in (1, 0):
        attend([(2, 1), (2, 2), (2, 3)], (H0,), sides=(side,), is_last=True)
    for side in (1, 0):
        attend([(2, 3)], (H1,), sides=(side,), is_last=True)

    for head in range(CORE_HEADS):
        output(head, 0).wait()
        output(head, 1).wait()
    for copy in swaps + started:
        copy.wait_send()


def copy_kernel(source, target, held, sems):
    parts = []
    for part in range(COPY_PARTS):
        rows = slice(part * 16, (part + 1) * 16)
        parts.append((
            pltpu.make_async_copy(source.at[0, rows], held.at[rows], sems.at[0, part]),
            pltpu.make_async_copy(held.at[rows], target.at[0, rows], sems.at[1, part])))
    for come, _ in parts:
        come.start()
    for come, leave in parts:
        come.wait()
        leave.start()
    for _, leave in parts:
        leave.wait()


def body(queries, keys, values, placement, lengths):
    any_spec = pl.BlockSpec(memory_space=pl.ANY)
    smem = pl.BlockSpec(memory_space=pltpu.SMEM)
    dma = pltpu.SemaphoreType.DMA
    out_shape = jax.ShapeDtypeStruct((1, TOK, KVH * GROUPS * HD), jnp.bfloat16)
    result = pl.pallas_call(
        kernel,
        out_shape=out_shape,
        in_specs=[any_spec, any_spec, any_spec, smem, smem],
        out_specs=any_spec,
        scratch_shapes=[
            pltpu.VMEM((3, NUM_X, 2, 2, CHIP_TOK, HALF_LANES), jnp.bfloat16),
            pltpu.VMEM((3, NUM_X, 32, TOK), jnp.int32),
            pltpu.VMEM((2, TOK, CORE_OUT), jnp.bfloat16),
            pltpu.VMEM((2, TOK, CORE_OUT), jnp.bfloat16),
            pltpu.VMEM((CORE_HEADS, 2, ROWS, 2 * HD), jnp.float32),
            pltpu.VMEM((CORE_HEADS, 2, ROWS, HD), jnp.float32),
            pltpu.VMEM((MAX_KEYS, HD), jnp.bfloat16),
            pltpu.VMEM((2, TILE, HD), jnp.bfloat16),
            dma((4, 2)),
            dma((7,)),
            dma((7,)),
            dma((3, CORE_HEADS)),
            dma((3, NUM_X, 5)),
            dma((2, NUM_X, 3)),
            dma((3, 2, 3, 5)),
            dma((6, 3)),
        ],
        compiler_params=pltpu.CompilerParams(
            collective_id=0, has_side_effects=True, vmem_limit_bytes=56 * 1024 * 1024),
        cost_estimate=pl.CostEstimate(
            flops=4 * TOK * 64 * 3072 * HD, bytes_accessed=5 * 1024 * 1024,
            transcendentals=TOK * 64 * 3072),
    )(queries, keys, values, placement, lengths)
    return pl.pallas_call(
        copy_kernel,
        out_shape=out_shape,
        in_specs=[any_spec],
        out_specs=any_spec,
        scratch_shapes=[
            pltpu.VMEM((TOK, KVH * GROUPS * HD), jnp.bfloat16),
            dma((2, COPY_PARTS)),
        ],
        compiler_params=pltpu.CompilerParams(vmem_limit_bytes=56 * 1024 * 1024),
    )(result)


def solution(mesh):
    in_specs = (
        P("grp", "ctx", None),
        P("grp", "ctx", None),
        P("grp", "ctx", None),
        P("grp", "ctx"),
        P(),
    )
    out_specs = P("grp", "ctx", None)
    return jax.shard_map(body, mesh=mesh, in_specs=in_specs, out_specs=out_specs, check_vma=False)
```

```python
import math

import jax
import jax.numpy as jnp
from jax import lax
from jax.experimental import pallas as pl
from jax.experimental.pallas import tpu as pltpu
from jax.sharding import PartitionSpec as P

HD = 128
KVH = 8
GROUPS = 8
STRETCH = 64
TOK = 128
COL_STRETCHES = 16
REQS = 32
NUM_X = 4
NUM_GRP = 32
ROWS = GROUPS * TOK
TILE = 512
CORE_HEADS = KVH // 2
HALF_HEADS = CORE_HEADS // 2
HALF_LANES = HALF_HEADS * HD
CORE_LANES = CORE_HEADS * HD
HEAD_OUT = GROUPS * HD
HALF_OUT = HALF_HEADS * HEAD_OUT
CORE_OUT = CORE_HEADS * GROUPS * HD
CHIP_TOK = 2 * TOK
MAX_KEYS = 768
COPY_PARTS = TOK // 16

HIDDEN = -2e30
SCALE = math.log2(math.e) / math.sqrt(HD)
MESH = pl.DeviceIdType.MESH
H0, H1, POS, K1, V1 = 0, 1, 2, 3, 4


def kernel(q_hbm, k_hbm, v_hbm, place_ref, len_ref, out_hbm,
           kvbuf, pbuf, q_vm, out_vm, acc, run_max, extra, which,
           local_sem, swap_send, swap_recv, out_sem, recv_ici, send_z, send_x, send_own):
    ctx = lax.axis_index("ctx")
    grp = lax.axis_index("grp")
    x = ctx // 2
    core = ctx % 2
    right = (((x + 1) % NUM_X) * 2 + core, grp)
    left = (((x + NUM_X - 1) % NUM_X) * 2 + core, grp)
    sibling = (x * 2 + 1 - core, grp)
    after = (ctx, (grp + 1) % NUM_GRP)
    before = (ctx, (grp + NUM_GRP - 1) % NUM_GRP)

    barrier = pltpu.get_barrier_semaphore()
    for device in (right, left, sibling, after, before):
        pl.semaphore_signal(barrier, inc=1, device_id=device, device_id_type=MESH)

    def lanes_of(which_core, half, core_lanes, half_lanes):
        start = which_core * core_lanes + half * half_lanes
        return pl.ds(pl.multiple_of(start, half_lanes), half_lanes)

    local = []
    for half in range(2):
        for part, source in enumerate((k_hbm, v_hbm)):
            local.append(pltpu.make_async_copy(
                source.at[0, :, lanes_of(core, half, CORE_LANES, HALF_LANES)],
                kvbuf.at[0, 0, half, part, 0:TOK], local_sem.at[half, part]))
    queries_in = []
    for half in range(2):
        queries_in.append(pltpu.make_async_copy(
            q_hbm.at[0, :, lanes_of(core, half, CORE_OUT, HALF_OUT)],
            q_vm.at[0, :, half * HALF_OUT:(half + 1) * HALF_OUT], local_sem.at[2, half]))
    for copy in local + queries_in:
        copy.start()

    for slot in range(2):
        pbuf[0, 0, 8 * slot:8 * slot + 8] = jnp.full(
            (8, TOK), grp * COL_STRETCHES + place_ref[0, slot], jnp.int32)

    pl.semaphore_wait(barrier, 5)

    started = []

    def remote(src, dst, send_sem, recv_sem, device):
        return pltpu.make_async_remote_copy(
            src_ref=src, dst_ref=dst, send_sem=send_sem, recv_sem=recv_sem,
            device_id=device, device_id_type=MESH)

    swaps = [remote(pbuf.at[0, 0, 0:16], pbuf.at[0, 0, 16:32], swap_send.at[0], swap_recv.at[0], sibling)]
    for half in range(2):
        for part, source in enumerate((k_hbm, v_hbm)):
            i = 1 + 2 * half + part
            swaps.append(remote(
                source.at[0, :, lanes_of(1 - core, half, CORE_LANES, HALF_LANES)],
                kvbuf.at[0, 0, half, part, TOK:CHIP_TOK], swap_send.at[i], swap_recv.at[i], sibling))
    for half in range(2):
        swaps.append(remote(
            q_hbm.at[0, :, lanes_of(1 - core, half, CORE_OUT, HALF_OUT)],
            q_vm.at[1, :, half * HALF_OUT:(half + 1) * HALF_OUT],
            swap_send.at[5 + half], swap_recv.at[5 + half], sibling))
    for swap in swaps[:5]:
        swap.start()

    def unit(kind, d, rx):
        if kind == POS:
            return pbuf.at[d, rx]
        if kind in (K1, V1):
            return kvbuf.at[d, rx, H1, kind - K1]
        return kvbuf.at[d, rx, kind]

    def send(kind, src, dst, sem, device):
        copy = remote(unit(kind, *src), unit(kind, *dst), sem, recv_ici.at[dst[0], dst[1], kind], device)
        copy.start()
        started.append(copy)

    def to_after(d, rx, kind):
        send(kind, (d, rx), (d + 1, rx), send_z.at[d, rx, kind], after)

    def to_right(d, rx, kind):
        send(kind, (d, rx), (d, 1 if rx == 0 else 3), send_x.at[d, 0, rx, kind], right)

    def to_left(d, rx, kind):
        send(kind, (d, rx), (d, 2 if rx == 0 else 3), send_x.at[d, 1, rx, kind], left)

    def own_tokens(i, half, dst, device):
        for part, source in enumerate((k_hbm, v_hbm)):
            copy = remote(
                source.at[0, :, lanes_of(core, half, CORE_LANES, HALF_LANES)],
                kvbuf.at[dst[0], dst[1], half, part, 0:TOK],
                send_own.at[i, part], recv_ici.at[dst[0], dst[1], half], device)
            copy.start()
            started.append(copy)

    def swapped_tokens(i, half, dst, device):
        copy = remote(
            kvbuf.at[0, 0, half, :, TOK:CHIP_TOK], kvbuf.at[dst[0], dst[1], half, :, TOK:CHIP_TOK],
            send_own.at[i, 2], recv_ici.at[dst[0], dst[1], half], device)
        copy.start()
        started.append(copy)

    own_sends = (
        (H0, (0, 1), right), (H0, (1, 0), after), (H1, (0, 2), left),
        (H1, (1, 0), after), (H1, (0, 1), right), (H0, (0, 2), left))
    for i in range(3):
        own_tokens(i, *own_sends[i])
    swaps[0].wait_recv()
    to_right(0, 0, POS)
    to_left(0, 0, POS)
    to_after(0, 0, POS)
    for part in range(2):
        swaps[1 + part].wait_recv()
    swapped_tokens(0, *own_sends[0])
    swapped_tokens(1, *own_sends[1])
    for part in range(2):
        swaps[3 + part].wait_recv()
    swapped_tokens(2, *own_sends[2])
    for swap in swaps[5:]:
        swap.start()
    for i in range(3, 6):
        own_tokens(i, *own_sends[i])
        swapped_tokens(i, *own_sends[i])
    for copy in local:
        copy.wait()

    waited = set()
    for kind in (POS, H0, H1):
        waited.add((0, 0, kind))

    def got(d, rx, kind):
        if (d, rx, kind) in waited:
            return
        waited.add((d, rx, kind))
        ref = unit(kind, d, rx)
        remote(ref, ref, local_sem.at[3, 0], recv_ici.at[d, rx, kind], sibling).wait_recv()
        if d == 1 and rx == 0:
            if kind == POS:
                to_right(1, 0, POS)
                to_left(1, 0, POS)
                to_after(1, 0, POS)
            elif kind == H0:
                to_right(1, 0, H0)
                to_after(1, 0, H0)
            else:
                to_left(1, 0, H1)
                to_after(1, 0, H1)
                to_right(1, 0, H1)
                to_left(1, 0, H0)
        elif d == 2 and rx == 0:
            if kind == POS:
                to_right(2, 0, POS)
                to_left(2, 0, POS)
            elif kind == H1:
                got(2, 0, H0)
                to_right(2, 0, H1)
                to_left(2, 0, H1)
                to_right(2, 0, H0)
                to_left(2, 0, H0)
        elif d == 0 and rx == 1 and kind in (POS, H0):
            to_right(0, 1, kind)
        elif d == 0 and rx == 2 and kind == H1:
            to_left(0, 2, H1)
        elif d == 0 and rx == 3:
            to_after(0, 3, kind)
        elif d == 1 and rx == 3 and kind in (POS, H0):
            to_after(1, 3, kind)
        elif d == 2 and rx == 1 and kind == H1:
            to_right(2, 1, K1)
        elif d == 2 and rx == 2 and kind == H1:
            to_left(2, 2, V1)

    lane = lax.broadcasted_iota(jnp.int32, (8, TOK), 1)
    highs = jnp.full((8, TOK), -1, jnp.int32)
    for t in range(4):
        highs = jnp.where(lane == t, pbuf[0, 0, 8 * t:8 * t + 8, :], highs)
    lows = jnp.zeros((8, TOK), jnp.int32)
    end = jnp.int32(0)
    for r in range(REQS):
        end = end + len_ref[r]
        lows = jnp.where(end <= highs, end, lows)

    token = lax.broadcasted_iota(jnp.int32, (TILE, HD), 0) % TOK
    column = lax.broadcasted_iota(jnp.int32, (TILE, HD), 1)
    for side in range(2):
        which[side] = jnp.where(token // STRETCH + 2 * side == column, 1.0, 0.0).astype(jnp.bfloat16)

    def causal():
        row = lax.broadcasted_iota(jnp.int32, (TOK, TOK), 0)
        col = lax.broadcasted_iota(jnp.int32, (TOK, TOK), 1)
        later = (row // STRETCH == col // STRETCH) & (col > row)
        return jnp.where(later, HIDDEN, 0.0)

    def attend(chunks, halves=(H0, H1), sides=(0, 1), is_first=False, is_last=False):
        for d, rx in chunks:
            for kind in (POS,) + halves:
                if (d, rx, kind) == (2, 3, H1):
                    got(2, 3, K1)
                    got(2, 3, V1)
                else:
                    got(d, rx, kind)
        num_keys = CHIP_TOK * len(chunks)
        for i, (d, rx) in enumerate(chunks):
            for t in range(4):
                stretch = pbuf[d, rx, 8 * t:8 * t + 8, :]
                hide = jnp.where((stretch >= lows) & (stretch <= highs), 0.0, HIDDEN)
                at = i * CHIP_TOK + t * STRETCH
                extra[at:at + STRETCH, :] = jnp.concatenate([hide] * 8, axis=0).astype(jnp.bfloat16)

        def load(half, inner):
            lanes = slice(inner * HD, (inner + 1) * HD)
            keys = jnp.concatenate([kvbuf[d, rx, half, 0, :, lanes] for d, rx in chunks], axis=0)
            vals = jnp.concatenate([kvbuf[d, rx, half, 1, :, lanes] for d, rx in chunks], axis=0)
            keys = jnp.concatenate([keys, extra[:num_keys, :]], axis=1)
            vals = jnp.concatenate([vals, jnp.ones_like(vals)], axis=1)
            return half * HALF_HEADS + inner, keys, vals

        def score(loaded, side, tile):
            head, keys, _ = loaded
            queries = []
            for j in range(TILE // TOK):
                group = tile * (TILE // TOK) + j
                lanes = pl.ds(pl.multiple_of((head * GROUPS + group) * HD, HD), HD)
                queries.append(q_vm[side, :, lanes])
            queries = jnp.concatenate([jnp.concatenate(queries, axis=0), which[side]], axis=1)
            return lax.dot_general(
                queries, keys, (((1,), (1,)), ((), ())), preferred_element_type=jnp.float32)

        def absorb(loaded, side, tile, scores):
            head, _, vals = loaded
            rows = slice(tile * TILE, (tile + 1) * TILE)
            if is_first:
                own = scores[:, side * TOK:(side + 1) * TOK]
                own = (own.reshape(TILE // TOK, TOK, TOK) + causal()[None]).reshape(TILE, TOK)
                both = (own, scores[:, TOK:]) if side == 0 else (scores[:, :TOK], own)
                scores = jnp.concatenate(both, axis=1)
            top = jnp.broadcast_to(jnp.max(scores, axis=1, keepdims=True), (TILE, HD)) * SCALE
            if not is_first:
                old = run_max[head, side, rows]
                top = jnp.maximum(old, top)
            tops = jnp.concatenate([top] * (num_keys // HD), axis=1)
            weights = jnp.exp2(scores * SCALE - tops).astype(jnp.bfloat16)
            part = lax.dot_general(
                weights, vals, (((1,), (0,)), ((), ())),
                preferred_element_type=jnp.float32)
            if not is_first:
                factor = jnp.exp2(old - top)
                part = part + acc[head, side, rows] * jnp.concatenate([factor, factor], axis=1)
            if is_last:
                result = (part[:, :HD] / part[:, HD:]).astype(jnp.bfloat16)
                for j in range(TILE // TOK):
                    group = tile * (TILE // TOK) + j
                    place = pl.ds(pl.multiple_of((head * GROUPS + group) * HD, HD), HD)
                    out_vm[side, :, place] = result[j * TOK:(j + 1) * TOK]
            else:
                acc[head, side, rows] = part
                run_max[head, side, rows] = top

        def some_heads(step, carry):
            half = halves[0] if len(halves) == 1 else step % 2
            side = sides[0] if len(sides) == 1 else step // len(halves)
            work = []
            for i in range(HALF_HEADS):
                loaded = load(half, i)
                work += [(loaded, side, tile) for tile in range(ROWS // TILE)]
            scores = score(*work[0])
            for i, item in enumerate(work):
                following = score(*work[i + 1]) if i + 1 < len(work) else None
                absorb(*item, scores)
                scores = following
                if is_last and item[2] == ROWS // TILE - 1:
                    output(item[0][0], side).start()
            return carry

        lax.fori_loop(0, len(halves) * len(sides), some_heads, 0)

    def output(head, side):
        source = out_vm.at[side, :, pl.ds(head * HEAD_OUT, HEAD_OUT)]
        target = out_hbm.at[0, :, lanes_of(core, head, CORE_OUT, HEAD_OUT)]
        if side == 0:
            return pltpu.make_async_copy(source, target, out_sem.at[0, head])
        return remote(source, target, out_sem.at[1, head], out_sem.at[2, head], sibling)

    for copy in queries_in:
        copy.wait()
    attend([(0, 0)], sides=(0,), is_first=True)
    got(0, 1, POS)
    got(0, 1, H0)
    got(0, 2, H1)
    got(1, 0, POS)
    got(1, 0, H0)
    for swap in swaps[5:]:
        swap.wait_recv()
    attend([(0, 0)], sides=(1,), is_first=True)
    got(1, 0, H1)
    attend([(0, 1), (0, 2), (1, 0)], (H1,))
    attend([(0, 1), (0, 2), (1, 0)], (H0,))
    for kind in (POS, H0, H1):
        got(0, 3, kind)
    for kind in (POS, H0, H1):
        got(2, 0, kind)
    attend([(0, 3), (2, 0), (1, 1)], (H0,))
    attend([(0, 3), (2, 0), (1, 2)], (H1,))
    attend([(1, 2), (1, 3)], (H0,))
    got(2, 1, POS)
    got(2, 2, POS)
    got(2, 1, H1)
    got(2, 2, H1)
    attend([(1, 1), (1, 3)], (H1,))
    attend([(2, 1), (2, 2)], (H1,))
    for side in (1, 0):
        attend([(2, 1), (2, 2), (2, 3)], (H0,), sides=(side,), is_last=True)
    for side in (1, 0):
        attend([(2, 3)], (H1,), sides=(side,), is_last=True)

    for head in range(CORE_HEADS):
        output(head, 0).wait()
        output(head, 1).wait()
    for copy in swaps + started:
        copy.wait_send()


def copy_kernel(source, target, held, sems):
    parts = []
    for part in range(COPY_PARTS):
        rows = slice(part * 16, (part + 1) * 16)
        parts.append((
            pltpu.make_async_copy(source.at[0, rows], held.at[rows], sems.at[0, part]),
            pltpu.make_async_copy(held.at[rows], target.at[0, rows], sems.at[1, part])))
    for come, _ in parts:
        come.start()
    for come, leave in parts:
        come.wait()
        leave.start()
    for _, leave in parts:
        leave.wait()


def body(queries, keys, values, placement, lengths):
    any_spec = pl.BlockSpec(memory_space=pl.ANY)
    smem = pl.BlockSpec(memory_space=pltpu.SMEM)
    dma = pltpu.SemaphoreType.DMA
    out_shape = jax.ShapeDtypeStruct((1, TOK, KVH * GROUPS * HD), jnp.bfloat16)
    result = pl.pallas_call(
        kernel,
        out_shape=out_shape,
        in_specs=[any_spec, any_spec, any_spec, smem, smem],
        out_specs=any_spec,
        scratch_shapes=[
            pltpu.VMEM((3, NUM_X, 2, 2, CHIP_TOK, HALF_LANES), jnp.bfloat16),
            pltpu.VMEM((3, NUM_X, 32, TOK), jnp.int32),
            pltpu.VMEM((2, TOK, CORE_OUT), jnp.bfloat16),
            pltpu.VMEM((2, TOK, CORE_OUT), jnp.bfloat16),
            pltpu.VMEM((CORE_HEADS, 2, ROWS, 2 * HD), jnp.float32),
            pltpu.VMEM((CORE_HEADS, 2, ROWS, HD), jnp.float32),
            pltpu.VMEM((MAX_KEYS, HD), jnp.bfloat16),
            pltpu.VMEM((2, TILE, HD), jnp.bfloat16),
            dma((4, 2)),
            dma((7,)),
            dma((7,)),
            dma((3, CORE_HEADS)),
            dma((3, NUM_X, 5)),
            dma((2, NUM_X, 3)),
            dma((3, 2, 3, 5)),
            dma((6, 3)),
        ],
        compiler_params=pltpu.CompilerParams(
            collective_id=0, has_side_effects=True, vmem_limit_bytes=56 * 1024 * 1024),
        cost_estimate=pl.CostEstimate(
            flops=4 * TOK * 64 * 3072 * HD, bytes_accessed=5 * 1024 * 1024,
            transcendentals=TOK * 64 * 3072),
    )(queries, keys, values, placement, lengths)
    return pl.pallas_call(
        copy_kernel,
        out_shape=out_shape,
        in_specs=[any_spec],
        out_specs=any_spec,
        scratch_shapes=[
            pltpu.VMEM((TOK, KVH * GROUPS * HD), jnp.bfloat16),
            dma((2, COPY_PARTS)),
        ],
        compiler_params=pltpu.CompilerParams(vmem_limit_bytes=56 * 1024 * 1024),
    )(result)


def solution(mesh):
    in_specs = (
        P("grp", "ctx", None),
        P("grp", "ctx", None),
        P("grp", "ctx", None),
        P("grp", "ctx"),
        P(),
    )
    out_specs = P("grp", "ctx", None)
    return jax.shard_map(body, mesh=mesh, in_specs=in_specs, out_specs=out_specs, check_vma=False)
```
